32 devices in a mesh: groups: 2 (over y), ctx: 4 (over z), head: 2 (over x), sess: 2 (over core).
Axes of the slice: x: 2, y: 2, z: 4, core: 2. Of those that a mesh axis runs over, the one named last changes fastest.
Arguments:
- head_input: bfloat16 [8, 512, 8192], P(('groups', 'sess'), 'ctx', 'head'), parts along dimension 0, may hold values from -6 to 6
- gate_input: bfloat16 [8, 512, 8192], P(('groups', 'sess'), 'ctx', 'head'), parts along dimension 0, may hold values from -6 to 6
- state_in_proj: bfloat16 [8, 512, 8, 128], P(('groups', 'sess'), 'ctx'), parts along dimension 0, may hold values from -1.796875 to 1.796875
- state_out_proj: bfloat16 [8, 512, 8, 128], P(('groups', 'sess'), 'ctx'), parts along dimension 0, may hold values from -1.796875 to 1.796875
- step_raw: float32 [8, 512, 128], P(('groups', 'sess'), 'ctx', 'head'), parts along dimension 0, may hold values from -2.5 to 12.5
- head_step_bias: float32 [128], P('head'), may hold values from -5.3 to -2.25
- decay_log: float32 [128], P('head'), may hold values from -7.7 to 0
- skip_gain: float32 [128], P('head'), may hold values from 0.5 to 2
- norm_gain: float32 [8192], P('head'), may hold values from 0.1 to 1.9
- out_weight: bfloat16 [8192, 4096], P('head', 'ctx'), may hold values from -0.09375 to 0.09375
- pool_states: float32 [16, 128, 64, 128], P(('groups', 'sess'), 'head', None, 'ctx'), parts along dimension 0, may hold values from -6 to 6
- slot_map: int32 [8], P('groups'), parts along dimension 0, may hold values from 0 to 7, as said below
- span_lengths: int32 [8], P('groups'), parts along dimension 0, may hold values from 1 to 4, as said below
Outputs:
- mixed: bfloat16 [8, 512, 4096], P(('groups', 'sess'), 'ctx', 'head'), parts along dimension 0
- final_states: float32 [8, 128, 64, 128], P(('groups', 'sess'), 'head', None, 'ctx'), parts along dimension 0
The draws below stay inside these ranges and needn't reach their ends.
There are 2 independent parts, one for each index of `groups`. The reference program is written for one: setup_inputs(seed, part) draws one part's arguments, and reference() takes and returns one part's arrays. A program takes and returns all parts, laid end to end along the dimension named above; an argument that names none is the same for every part. Nothing has to cross between parts.
Inputs may be any that keep to these rules, and one draw needn't show every extreme that they name: `slot_map`: the sessions of a group take distinct decode slots. `span_lengths`: some session of every group fills all 4 units.
All inputs are finite; a program needn't handle non-finite values.
Results may differ from the reference program's by a relative error of at most 0.018.
Values may be sent and summed in bfloat16 or wider, within the bound.
No kernel may reach another device: no remote copies, remote signals or barrier semaphores. Data moves between devices by JAX's collectives and lax.ppermute only.
A program may use at most 128 MiB of HBM per device.

```python
import math
import jax
import jax.numpy as jnp
from jax import lax

D_WIN = 4096
HEADS = 128
HEAD_DIM = 64
STATE = 128
GROUPS = 8
SPAN = 128
SESS_DEV = 2
RESULT_LENGTH = 512
SPANS = 4
GROUP_SESSIONS = 4
SLOTS = 8
N_HEAD = 2


def draw_step_raw(key, part):
    base_key = jax.random.fold_in(key, 11)
    flurry_random_key = jax.random.fold_in(key, 12)
    starting_values = jnp.clip(0.5 * jax.random.normal(base_key, (GROUP_SESSIONS, RESULT_LENGTH, HEADS), jnp.float32), -2.5, 2.5)
    flurry_lengths = (jax.random.randint(flurry_random_key, (GROUP_SESSIONS, RESULT_LENGTH, 1), 0, 1024) == 0).astype(jnp.float32)
    return starting_values + 10.0 * flurry_lengths


def draw_decay_log(key, part):
    rate_key = jax.random.fold_in(key, 21)
    return jax.random.uniform(rate_key, (HEADS,), jnp.float32, math.log(0.001), 0.0)


def draw_slot_map(key, part):
    middle = (jax.random.permutation(jax.random.fold_in(key, 31), SLOTS - 2)[:GROUP_SESSIONS - 2] + 1).astype(jnp.int32)
    high_session = jax.random.randint(jax.random.fold_in(key, 33), (), 0, SESS_DEV)
    low_session = GROUP_SESSIONS - SESS_DEV + jax.random.randint(jax.random.fold_in(key, 34), (), 0, SESS_DEV)
    index_values = jnp.arange(GROUP_SESSIONS, dtype=jnp.int32)
    special = (index_values == high_session) | (index_values == low_session)
    others_rank = jnp.cumsum(jnp.where(special, 0, 1)) - 1
    others_rank = jnp.clip(others_rank, 0, GROUP_SESSIONS - 3).astype(jnp.int32)
    filled = middle[others_rank]
    result = jnp.where(index_values == high_session, SLOTS - 1, jnp.where(index_values == low_session, 0, filled))
    return result.astype(jnp.int32)


def draw_span_lengths(key, part):
    base_len = jax.random.randint(jax.random.fold_in(key, 41), (GROUP_SESSIONS,), 1, SPANS + 1)
    full_one = jax.random.randint(jax.random.fold_in(key, 42), (), 0, GROUP_SESSIONS)
    return jnp.where(jnp.arange(GROUP_SESSIONS) == full_one, SPANS, base_len).astype(jnp.int32)


def strengthened(values, stream_key, source, target, shards_of, factor):
    def block_of(dim):
        return (jnp.arange(values.shape[dim]) // (values.shape[dim] // shards_of)).reshape((-1,) + (1,) * (values.ndim - 1 - dim))

    first = jax.random.permutation(stream_key, shards_of)[block_of(target)]
    far = (block_of(target) + shards_of // 2) % shards_of
    return jnp.where((block_of(source) == first) | (block_of(source) == far), factor * values, values)


def shard_levels(key, dims, pieces, least, high):
    def one(axis_at, blocks):
        draws = jax.random.uniform(jax.random.fold_in(jax.random.fold_in(key, 6), axis_at), (blocks,), jnp.float32, least / len(pieces), high / len(pieces))
        return jnp.repeat(jnp.exp(draws), dims[axis_at] // blocks).reshape((-1,) + (1,) * (len(dims) - axis_at - 1))

    gain = one(*pieces[0])
    for cut in pieces[1:]:
        gain = gain * one(*cut)
    return gain


def bell_draw(stream_key, extent, scale, limit, cuts=(), held_as=jnp.bfloat16):
    array = scale * jax.random.normal(stream_key, extent, jnp.float32)
    if cuts:
        array = array * shard_levels(stream_key, extent, cuts, -0.22, 0.18)
    return jnp.clip(array, -limit, limit).astype(held_as)


def gaussian_with(own_key, shape, deviation, reach, shards, heavy, kind=jnp.bfloat16):
    values = deviation * jax.random.normal(own_key, shape, jnp.float32)
    if shards:
        values = values * shard_levels(own_key, shape, shards, -0.22, 0.18)
    return jnp.clip(strengthened(values, jax.random.fold_in(own_key, 3), *heavy), -reach, reach).astype(kind)


def setup_inputs(seed: int = 0, part: int = 0) -> dict:
    splits = jax.random.split(jax.random.key(seed), 14)
    part_splits = jax.random.split(jax.random.fold_in(splits[13], part), 14)
    return {
        "head_input": bell_draw(part_splits[0], (GROUP_SESSIONS, RESULT_LENGTH, HEADS * HEAD_DIM), 1.0, 6.0, ((0, 2), (1, 4), (2, 2))),
        "gate_input": bell_draw(part_splits[1], (GROUP_SESSIONS, RESULT_LENGTH, HEADS * HEAD_DIM), 1.0, 6.0, ((0, 2), (1, 4), (2, 2))),
        "state_in_proj": bell_draw(part_splits[2], (GROUP_SESSIONS, RESULT_LENGTH, GROUPS, STATE), 0.3, 1.796875, ((0, 2), (1, 4))),
        "state_out_proj": bell_draw(part_splits[3], (GROUP_SESSIONS, RESULT_LENGTH, GROUPS, STATE), 0.3, 1.796875, ((0, 2), (1, 4))),
        "step_raw": draw_step_raw(jax.random.fold_in(jax.random.fold_in(splits[13], part), 71), part),
        "head_step_bias": jnp.clip(-5.3 + 3.0500002 * jax.random.uniform(splits[5], (HEADS,), jnp.float32) ** shard_levels(splits[5], (HEADS,), ((0, 2),), -0.2, 0.2), -5.3, -2.25),
        "decay_log": draw_decay_log(jax.random.fold_in(splits[13], 71), part),
        "skip_gain": jnp.clip(0.5 + 1.5 * jax.random.uniform(splits[7], (HEADS,), jnp.float32) ** shard_levels(splits[7], (HEADS,), ((0, 2),), -0.2, 0.2), 0.5, 2.0),
        "norm_gain": jnp.clip(1.0 + 0.18 * jax.random.normal(splits[8], (HEADS * HEAD_DIM,), jnp.float32), 0.1, 1.9),
        "out_weight": gaussian_with(splits[9], (HEADS * HEAD_DIM, D_WIN), (HEADS * HEAD_DIM) ** -0.5, 0.09375, ((0, 2), (1, 4)), (0, 1, 4, 2.0)),
        "pool_states": bell_draw(part_splits[10], (SLOTS, HEADS, HEAD_DIM, STATE), 1.0, 6.0, ((0, 2), (1, 2), (3, 4)), jnp.float32),
        "slot_map": draw_slot_map(jax.random.fold_in(jax.random.fold_in(splits[13], part), 71), part),
        "span_lengths": draw_span_lengths(jax.random.fold_in(jax.random.fold_in(splits[13], part), 71), part),
    }


def reference(head_input, gate_input, state_in_proj, state_out_proj, step_raw, head_step_bias, decay_log, skip_gain, norm_gain, out_weight, pool_states, slot_map, span_lengths):
    group_heads = HEADS // GROUPS
    position = jnp.arange(RESULT_LENGTH, dtype=jnp.int32)
    decay_rate = jnp.exp(decay_log)
    block_rows = HEADS * HEAD_DIM // N_HEAD
    mixed_rows = []
    final_rows = []
    for session in range(GROUP_SESSIONS):
        live_rows = (position < span_lengths[session] * SPAN).astype(jnp.float32)
        step_size = jax.nn.softplus(step_raw[session] + head_step_bias[None, :]) * live_rows[:, None]
        keep_rows = jnp.exp(-decay_rate[None, :] * step_size)
        inputs = head_input[session].astype(jnp.float32).reshape(RESULT_LENGTH, HEADS, HEAD_DIM)

        def advance(carried, stepped):
            x_token, b_token, c_token, size_token, keep_token = stepped
            b_heads = jnp.repeat(b_token.astype(jnp.float32), group_heads, axis=0)
            c_heads = jnp.repeat(c_token.astype(jnp.float32), group_heads, axis=0)
            carried = keep_token[:, None, None] * carried + (size_token[:, None] * x_token)[:, :, None] * b_heads[:, None, :]
            return (carried, lax.optimization_barrier(jnp.sum(carried * c_heads[:, None, :], axis=2)))
        start_state = pool_states[slot_map[session]]
        final_state, outputs = lax.scan(advance, start_state, (inputs, state_in_proj[session], state_out_proj[session], step_size, keep_rows))
        ssd_out = outputs + skip_gain[None, :, None] * inputs
        gated = ssd_out.reshape(RESULT_LENGTH, HEADS * HEAD_DIM) * jax.nn.silu(gate_input[session].astype(jnp.float32))
        grouped = gated.reshape(RESULT_LENGTH, GROUPS, group_heads * HEAD_DIM)
        norm_scale = lax.rsqrt(lax.optimization_barrier(jnp.mean(grouped * grouped, axis=2, keepdims=True)) + 1e-05)
        normed = ((grouped * norm_scale).reshape(RESULT_LENGTH, HEADS * HEAD_DIM) * norm_gain).astype(jnp.bfloat16)
        summed = jnp.zeros((RESULT_LENGTH, D_WIN), jnp.float32)
        for block_index in range(N_HEAD):
            low = block_index * block_rows
            partial_term = jnp.dot(normed[:, low:low + block_rows], out_weight[low:low + block_rows], preferred_element_type=jnp.float32)
            partial_term = lax.optimization_barrier(partial_term.astype(jnp.bfloat16))
            summed = summed + partial_term.astype(jnp.float32)
        mixed_rows.append((summed * live_rows[:, None]).astype(jnp.bfloat16))
        final_rows.append(final_state)
    return (jnp.stack(mixed_rows), jnp.stack(final_rows))
```

```python
import functools

import jax
import jax.numpy as jnp
from jax import lax
from jax.experimental import pallas as pl
from jax.experimental.pallas import tpu as pltpu
from jax.sharding import PartitionSpec as P

HEADS = 128
GROUPS = 8
SPAN = 128
GROUP_HEADS = HEADS // GROUPS
PIECES = 2

norm_eps = 1e-05
far = -1e30


def spread(values, head_dim):
    heads = values.shape[1]
    high = values.astype(jnp.bfloat16)
    low = (values - high.astype(jnp.float32)).astype(jnp.bfloat16)
    both = jnp.concatenate([high, low], axis=1)
    row = lax.broadcasted_iota(jnp.int32, (2 * heads, heads * head_dim), 0)
    col = lax.broadcasted_iota(jnp.int32, (2 * heads, heads * head_dim), 1)
    ones = (col // head_dim == row % heads).astype(jnp.bfloat16)
    return jnp.dot(both, ones, preferred_element_type=jnp.float32)


def local_kernel(
    limit_ref,
    x_ref,
    b_ref,
    c_ref,
    raw_ref,
    raw_t_ref,
    bias_ref,
    bias_t_ref,
    rate_ref,
    rate_t_ref,
    skip_ref,
    y_ref,
    end_ref,
    keep_ref,
    grow_ref,
):
    tokens, width = x_ref.shape[1:]
    heads = raw_ref.shape[3]
    head_dim = width // heads
    limit = limit_ref[pl.program_id(0)]
    token = lax.broadcasted_iota(jnp.int32, (tokens, heads), 0)
    token_t = lax.broadcasted_iota(jnp.int32, (heads, tokens), 1)
    size = jax.nn.softplus(raw_ref[0, 0] + bias_ref[0]) * (token < limit).astype(jnp.float32)
    size_t = jax.nn.softplus(raw_t_ref[0, 0] + bias_t_ref[0]) * (token_t < limit).astype(
        jnp.float32
    )
    log_keep = -jnp.exp(rate_ref[0]) * size
    log_keep_t = -jnp.exp(rate_t_ref[0]) * size_t
    row = lax.broadcasted_iota(jnp.int32, (tokens, tokens), 0)
    col = lax.broadcasted_iota(jnp.int32, (tokens, tokens), 1)
    causal = row >= col
    cum = jnp.dot(
        causal.astype(jnp.float32), log_keep, precision=lax.Precision.HIGHEST
    )
    cum_t = jnp.dot(
        log_keep_t, (row <= col).astype(jnp.float32), precision=lax.Precision.HIGHEST
    )
    shift_t = cum_t - jnp.where(size_t > 0, jnp.log(jnp.where(size_t > 0, size_t, 1.0)), far)
    b = b_ref[0, 0]
    scores = lax.dot_general(
        c_ref[0, 0], b, (((1,), (1,)), ((), ())), preferred_element_type=jnp.float32
    )
    lane = lax.broadcasted_iota(jnp.int32, (tokens, 2 * head_dim), 1)
    for pair in range(heads // 2):
        decayed = []
        for head in (2 * pair, 2 * pair + 1):
            gap = cum[:, head : head + 1] - shift_t[head : head + 1, :]
            decayed.append((scores * jnp.exp(jnp.where(causal, gap, far))).astype(jnp.bfloat16))
        here = pl.ds(pair * 2 * head_dim, 2 * head_dim)
        x = x_ref[0, :, here]
        zero = jnp.zeros_like(x)
        apart = jnp.concatenate(
            [jnp.where(lane < head_dim, x, zero), jnp.where(lane >= head_dim, x, zero)], axis=0
        )
        y = jnp.dot(
            jnp.concatenate(decayed, axis=1), apart, preferred_element_type=jnp.float32
        )
        y_ref[0, :, here] = y + skip_ref[0, :, here] * x.astype(jnp.float32)
    last = cum[tokens - 1 : tokens, :]
    tail = spread(jnp.exp(last - cum) * size, head_dim)
    weighted = (tail * x_ref[0].astype(jnp.float32)).astype(jnp.bfloat16)
    b_t = b.astype(jnp.float32).T.astype(jnp.bfloat16)
    end_ref[0, 0] = jnp.dot(b_t, weighted, preferred_element_type=jnp.float32)
    keep_ref[0, 0] = spread(jnp.broadcast_to(jnp.exp(last), (8, heads)), head_dim)
    grow_ref[0, 0] = jnp.exp(cum)


def norm_kernel(place_ref, state_ref, c_ref, grow_ref, y_ref, gate_ref, gain_ref, out_ref):
    width = y_ref.shape[2]
    heads = grow_ref.shape[3]
    from_state = jnp.dot(c_ref[0, 0], state_ref[0, 0], preferred_element_type=jnp.float32)
    ssd_out = y_ref[0] + from_state * spread(grow_ref[0, 0], width // heads)
    gate = gate_ref[0].astype(jnp.float32)
    gated = ssd_out * (gate / (1.0 + jnp.exp(-gate)))
    scale = lax.rsqrt(jnp.mean(gated * gated, axis=1, keepdims=True) + norm_eps)
    out_ref[0] = (gated * scale * gain_ref[0]).astype(jnp.bfloat16)


def local_part(limits, x, b, c, raw, bias, rate, skip):
    sessions, tokens, inner = x.shape
    groups = b.shape[1]
    state = b.shape[3]
    heads = raw.shape[3]
    width = inner // groups

    def by_group(*block):
        return pl.BlockSpec((1, *block), lambda s, g, _: (g, 0, 0))

    def by_both(*block):
        return pl.BlockSpec((1, 1, *block), lambda s, g, _: (s, g, 0, 0))

    def by_turn(*block):
        return pl.BlockSpec((1, 1, *block), lambda s, g, _: (g, s, 0, 0))

    flat = pl.BlockSpec((1, tokens, width), lambda s, g, _: (s, 0, g))
    f32 = jnp.float32
    return pl.pallas_call(
        local_kernel,
        grid_spec=pltpu.PrefetchScalarGridSpec(
            num_scalar_prefetch=1,
            grid=(sessions, groups),
            in_specs=[
                flat,
                by_both(tokens, state),
                by_both(tokens, state),
                by_both(tokens, heads),
                by_both(heads, tokens),
                by_group(1, heads),
                by_group(heads, 1),
                by_group(1, heads),
                by_group(heads, 1),
                by_group(1, width),
            ],
            out_specs=[
                flat,
                by_turn(state, width),
                by_turn(8, width),
                by_both(tokens, heads),
            ],
        ),
        out_shape=[
            jax.ShapeDtypeStruct((sessions, tokens, inner), f32),
            jax.ShapeDtypeStruct((groups, sessions, state, width), f32),
            jax.ShapeDtypeStruct((groups, sessions, 8, width), f32),
            jax.ShapeDtypeStruct((sessions, groups, tokens, heads), f32),
        ],
        compiler_params=pltpu.CompilerParams(vmem_limit_bytes=32 * 1024 * 1024),
        cost_estimate=pl.CostEstimate(
            flops=4 * 10**9, bytes_accessed=14 * 2**20, transcendentals=2**22
        ),
        name="local_part",
    )(
        limits,
        x,
        b,
        c,
        raw,
        raw.swapaxes(2, 3),
        bias[:, None, :],
        bias[:, :, None],
        rate[:, None, :],
        rate[:, :, None],
        skip,
    )


def normed_part(places, states, c, grow, y, gate, gain):
    sessions, tokens, inner = y.shape
    groups = c.shape[1]
    state = c.shape[3]
    heads = grow.shape[3]
    width = inner // groups
    flat = pl.BlockSpec((1, tokens, width), lambda s, g, _: (s, 0, g))
    return pl.pallas_call(
        norm_kernel,
        grid_spec=pltpu.PrefetchScalarGridSpec(
            num_scalar_prefetch=1,
            grid=(sessions, groups),
            in_specs=[
                pl.BlockSpec((1, 1, state, width), lambda s, g, place: (place[g], s, 0, 0)),
                pl.BlockSpec((1, 1, tokens, state), lambda s, g, _: (s, g, 0, 0)),
                pl.BlockSpec((1, 1, tokens, heads), lambda s, g, _: (s, g, 0, 0)),
                flat,
                flat,
                pl.BlockSpec((1, 1, width), lambda s, g, _: (g, 0, 0)),
            ],
            out_specs=flat,
        ),
        out_shape=jax.ShapeDtypeStruct((sessions, tokens, inner), jnp.bfloat16),
        compiler_params=pltpu.CompilerParams(vmem_limit_bytes=32 * 1024 * 1024),
        cost_estimate=pl.CostEstimate(
            flops=5 * 10**8, bytes_accessed=12 * 2**20, transcendentals=2**21
        ),
        name="normed_part",
    )(places, states, c, grow, y, gate, gain)


def shards(
    head_input,
    gate_input,
    state_in_proj,
    state_out_proj,
    step_raw,
    head_step_bias,
    decay_log,
    skip_gain,
    norm_gain,
    out_weight,
    pool_states,
    slot_map,
    span_lengths,
):
    turns = lax.axis_size("ctx")
    turn = lax.axis_index("ctx")
    lanes = lax.axis_size("groups")
    lane = lax.axis_index("groups")
    cores = lax.axis_size("sess")
    core = lax.axis_index("sess")
    head_count = lax.axis_size("head")
    head_index = lax.axis_index("head")
    sessions, tokens, inner = head_input.shape
    heads = step_raw.shape[2]
    head_dim = inner // heads
    slots = pool_states.shape[0]
    state_cols = pool_states.shape[3]
    groups = heads // GROUP_HEADS
    width = inner // groups
    bf16 = jnp.bfloat16

    def columns_of(slot):
        held = lax.dynamic_index_in_dim(pool_states, slot % slots, 0, keepdims=False)
        held = held.astype(bf16).transpose(2, 0, 1)
        return held.reshape(state_cols, groups, width).transpose(1, 0, 2)

    def slots_of(which):
        return lax.dynamic_slice_in_dim(slot_map, which * sessions, sessions)

    own_slots = slots_of(core)
    start = jnp.zeros((groups, sessions, state_cols, width), bf16)
    for by in range(cores):
        asked = slots_of((core - by) % cores)
        found = jnp.stack([columns_of(asked[s]) for s in range(sessions)], axis=1)
        if by:
            found = lax.ppermute(found, "sess", [(i, (i - by) % cores) for i in range(cores)])
            holder = (core + by) % cores
        else:
            holder = core
        here = (own_slots // slots == holder)[None, :, None, None]
        start = jnp.where(here, found, start)
    columns = [start]
    for other in range(1, turns):
        columns.append(lax.ppermute(start, "ctx", [(other, 0)]))
    first_state = jnp.concatenate(columns, axis=2)

    carriers = lanes * cores
    rows = inner // carriers
    carrier = lane * cores + core
    mine = lax.dynamic_slice_in_dim(out_weight, carrier * rows, rows, 0)
    piece_rows = rows // PIECES

    def share(block, holders):
        got = {(0, 0): block}
        for by in range(1, lanes):
            pairs = [
                (y * turns + z, (y - by) % lanes * turns + z) for y in range(lanes) for z in holders
            ]
            got[by, 0] = lax.ppermute(block, ("groups", "ctx"), pairs)
        for by_lane in range(lanes):
            for by in range(1, cores):
                pairs = [
                    (z * cores + c, z * cores + (c - by) % cores)
                    for z in holders
                    for c in range(cores)
                ]
                got[by_lane, by] = lax.ppermute(got[by_lane, 0], ("ctx", "sess"), pairs)
        return got

    up = {}
    down = {}
    for piece in range(PIECES):
        block = mine[piece * piece_rows : (piece + 1) * piece_rows]
        ahead = back = block
        for hop in range(1, turns):
            ahead = lax.ppermute(ahead, "ctx", [(i, i + 1) for i in range(hop - 1, turns - 1)])
            back = lax.ppermute(back, "ctx", [(i + 1, i) for i in range(turns - hop)])
            up[hop, piece] = share(ahead, range(hop, turns))
            down[hop, piece] = share(back, range(turns - hop))

    first_session = core * sessions
    own_lengths = lax.dynamic_slice_in_dim(span_lengths, first_session, sessions)
    limits = jnp.clip(own_lengths * SPAN - turn * tokens, 0, tokens)
    first_group = head_index * groups

    def grouped(proj):
        return lax.dynamic_slice_in_dim(proj, first_group, groups, 2).swapaxes(1, 2)

    b = grouped(state_in_proj)
    c = grouped(state_out_proj)
    raw = step_raw.reshape(sessions, tokens, groups, GROUP_HEADS).swapaxes(1, 2)
    skip = jnp.repeat(skip_gain, head_dim).reshape(groups, 1, width)
    y, local_end, keep, grow = local_part(
        limits,
        head_input,
        b,
        c,
        raw,
        head_step_bias.reshape(groups, GROUP_HEADS),
        decay_log.reshape(groups, GROUP_HEADS),
        skip,
    )

    waves = groups + turns - 2
    arrived = []
    coming = first_state[0]
    for wave in range(waves):
        at = jnp.clip(wave - turn, 0, groups - 1)
        if wave < groups:
            coming = jnp.where(turn == 0, first_state[wave], coming)
        gone = lax.dynamic_index_in_dim(keep, at, 0, keepdims=False)[:, :1]
        added = lax.dynamic_index_in_dim(local_end, at, 0, keepdims=False)
        leaving = (gone * coming.astype(jnp.float32) + added).astype(bf16)
        pairs = [(i, i + 1) for i in range(turns - 1) if 0 <= wave - i < groups]
        coming = lax.ppermute(leaving, "ctx", pairs)
        arrived.append(coming)
    states = jnp.concatenate([first_state, jnp.stack(arrived)], axis=0)
    places = jnp.arange(groups, dtype=jnp.int32)
    places = places + jnp.where(turn == 0, 0, groups + turn - 1)

    own_states = lax.dynamic_slice_in_dim(states, places[0], groups, 0)
    ended = (keep[:, :, :1] * own_states.astype(jnp.float32) + local_end).astype(bf16)
    final = ended[:, :, (turns - 1) * state_cols :]
    for other in range(turns - 1):
        part = ended[:, :, other * state_cols : (other + 1) * state_cols]
        part = lax.ppermute(part, "ctx", [(turns - 1, other)])
        final = jnp.where(turn == other, part, final)
    final = final.transpose(1, 2, 0, 3).reshape(sessions, state_cols, heads, head_dim)
    final_states = final.astype(jnp.float32).transpose(0, 2, 3, 1)

    normed = normed_part(
        places, states, c, grow, y, gate_input, norm_gain.reshape(groups, 1, width)
    ).reshape(sessions * tokens, inner)

    def product(parts):
        total = 0.0
        for by_lane in range(lanes):
            for by in range(cores):
                owner = (lane + by_lane) % lanes * cores + (core + by) % cores
                for piece in range(PIECES):
                    at = owner * rows + piece * piece_rows
                    left = lax.dynamic_slice_in_dim(normed, at, piece_rows, 1)
                    total = total + jnp.dot(
                        left, parts[piece][by_lane, by], preferred_element_type=jnp.float32
                    )
        return total

    blocks = [jnp.dot(normed, out_weight, preferred_element_type=jnp.float32).astype(bf16)]
    for by in range(1, turns):
        from_up = product([up[turns - by, piece] for piece in range(PIECES)])
        from_down = product([down[by, piece] for piece in range(PIECES)])
        blocks.append(jnp.where(turn + by < turns, from_down, from_up).astype(bf16))
    blocks = jnp.stack(blocks)
    blocks = lax.dynamic_slice_in_dim(
        jnp.concatenate([blocks, blocks], axis=0), (turns - turn) % turns, turns, 0
    )
    partial = blocks.transpose(1, 0, 2).reshape(sessions, tokens, -1)
    if head_count == 2:
        share_cols = partial.shape[2] // 2
        halves = partial.reshape(sessions, tokens, 2, share_cols)
        other = lax.dynamic_index_in_dim(halves, 1 - head_index, 2, keepdims=False)
        own = lax.dynamic_index_in_dim(halves, head_index, 2, keepdims=False)
        other = lax.ppermute(other, "head", [(0, 1), (1, 0)])
        summed = own.astype(jnp.float32) + other.astype(jnp.float32)
    else:
        summed = lax.psum_scatter(partial, "head", scatter_dimension=2, tiled=True).astype(
            jnp.float32
        )
    live = (jnp.arange(tokens, dtype=jnp.int32)[None, :] < limits[:, None]).astype(jnp.float32)
    mixed = (summed * live[:, :, None]).astype(bf16)
    return (mixed, final_states)


def solution(mesh):
    placed = (
        P(("groups", "sess"), "ctx", "head"),
        P(("groups", "sess"), "ctx", "head"),
        P(("groups", "sess"), "ctx", None, None),
        P(("groups", "sess"), "ctx", None, None),
        P(("groups", "sess"), "ctx", "head"),
        P("head"),
        P("head"),
        P("head"),
        P("head"),
        P("head", "ctx"),
        P(("groups", "sess"), "head", None, "ctx"),
        P("groups"),
        P("groups"),
    )
    return jax.shard_map(
        shards,
        mesh=mesh,
        in_specs=placed,
        out_specs=(
            P(("groups", "sess"), "ctx", "head"),
            P(("groups", "sess"), "head", None, "ctx"),
        ),
        check_vma=False,
    )
```

```python
import functools

import jax
import jax.numpy as jnp
from jax import lax
from jax.experimental import pallas as pl
from jax.experimental.pallas import tpu as pltpu
from jax.sharding import PartitionSpec as P

HEADS = 128
GROUPS = 8
SPAN = 128
GROUP_HEADS = HEADS // GROUPS
SPLIT = (1, 1)
TILE = 512
VMEM = 20 * 1024 * 1024

norm_eps = 1e-05
far = -1e30


def spread(values, head_dim):
    heads = values.shape[1]
    high = values.astype(jnp.bfloat16)
    low = (values - high.astype(jnp.float32)).astype(jnp.bfloat16)
    both = jnp.concatenate([high, low], axis=1)
    row = lax.broadcasted_iota(jnp.int32, (2 * heads, heads * head_dim), 0)
    col = lax.broadcasted_iota(jnp.int32, (2 * heads, heads * head_dim), 1)
    ones = (col // head_dim == row % heads).astype(jnp.bfloat16)
    return jnp.dot(both, ones, preferred_element_type=jnp.float32)


def local_kernel(
    limit_ref, x_ref, b_ref, c_ref, raw_ref, bias_ref, rate_ref, skip_ref, y_ref, end_ref, keep_ref, grow_ref
):
    tokens, width = x_ref.shape[1:]
    heads = raw_ref.shape[2]
    head_dim = width // heads
    f32 = jnp.float32
    token = lax.broadcasted_iota(jnp.int32, (heads, tokens), 1)
    size = jax.nn.softplus(raw_ref[0, 0] + bias_ref[0])
    size = size * (token < limit_ref[pl.program_id(0)]).astype(f32)
    log_keep = -jnp.exp(rate_ref[0]) * size
    row = lax.broadcasted_iota(jnp.int32, (tokens, tokens), 0)
    col = lax.broadcasted_iota(jnp.int32, (tokens, tokens), 1)
    causal = row >= col
    cum = jnp.dot(log_keep, (row <= col).astype(f32), precision=lax.Precision.HIGHEST)
    cum_t = cum.T
    shifted = cum - jnp.where(size > 0, jnp.log(jnp.where(size > 0, size, 1.0)), far)
    b = b_ref[0, 0]
    scores = lax.dot_general(
        c_ref[0, 0], b, (((1,), (1,)), ((), ())), preferred_element_type=f32
    )
    lane = lax.broadcasted_iota(jnp.int32, (tokens, 2 * head_dim), 1)
    for pair in range(heads // 2):
        decayed = []
        for head in (2 * pair, 2 * pair + 1):
            gap = cum_t[:, head : head + 1] - shifted[head : head + 1, :]
            decayed.append((scores * jnp.exp(jnp.where(causal, gap, far))).astype(jnp.bfloat16))
        here = pl.ds(pair * 2 * head_dim, 2 * head_dim)
        x = x_ref[0, :, here]
        zero = jnp.zeros_like(x)
        apart = jnp.concatenate(
            [jnp.where(lane < head_dim, x, zero), jnp.where(lane >= head_dim, x, zero)], axis=0
        )
        y = jnp.dot(jnp.concatenate(decayed, axis=1), apart, preferred_element_type=f32)
        y_ref[0, :, here] = y + skip_ref[0, :, here] * x.astype(f32)
    last = cum[:, tokens - 1 : tokens]
    tail = spread((jnp.exp(last - cum) * size).T, head_dim)
    weighted = (tail * x_ref[0].astype(f32)).astype(jnp.bfloat16)
    b_t = b.astype(f32).T.astype(jnp.bfloat16)
    end_ref[0, 0] = jnp.dot(b_t, weighted, preferred_element_type=f32)
    grow = jnp.exp(cum_t)
    keep_ref[0, 0] = spread(jnp.broadcast_to(grow[tokens - 1 :], (8, heads)), head_dim)
    grow_ref[0, 0] = grow


def leave_kernel(count, kind, *refs):
    at_ref, refs = refs[0], refs[1:]
    keep_ref, end_ref, state_ref, leaving_ref = refs[-4:]
    state = None
    if kind != "only":
        state = refs[0][0].astype(jnp.float32)
        refs = refs[1:]
    if count:
        first = jnp.concatenate([r[0, 0].astype(jnp.float32) for r in refs[:count]], axis=0)
        state = first if state is None else jnp.where(at_ref[1] == 0, first, state)
    state_ref[0] = state.astype(jnp.bfloat16)
    leaving_ref[0] = (keep_ref[0, 0, :1] * state + end_ref[0, 0]).astype(jnp.bfloat16)


def leave_part(at, coming, first, inside, keep, end):
    groups, sessions, state_size, width = end.shape
    by_turn = lambda s, at: (at[0], s, 0, 0)
    whole = pl.BlockSpec((1, state_size, width), lambda s, at: (s, 0, 0))
    operands, specs = [], []
    if coming is not None:
        operands.append(coming)
        specs.append(whole)
    if first is not None:
        operands += first
        specs += [
            pl.BlockSpec((1, 1, *f.shape[2:]), lambda s, at: (inside, s, 0, 0)) for f in first
        ]
    operands += [keep, end]
    specs += [
        pl.BlockSpec((1, 1, *keep.shape[2:]), by_turn),
        pl.BlockSpec((1, 1, state_size, width), by_turn),
    ]
    kind = None if first is None else ("only" if coming is None else "both")
    shape = jax.ShapeDtypeStruct((sessions, state_size, width), jnp.bfloat16)
    return pl.pallas_call(
        functools.partial(leave_kernel, 0 if first is None else len(first), kind),
        grid_spec=pltpu.PrefetchScalarGridSpec(
            num_scalar_prefetch=1, grid=(sessions,), in_specs=specs, out_specs=[whole, whole]
        ),
        out_shape=[shape, shape],
        compiler_params=pltpu.CompilerParams(vmem_limit_bytes=VMEM),
        cost_estimate=pl.CostEstimate(flops=10**6, bytes_accessed=3 * 2**20, transcendentals=0),
        name="leave_part",
    )(at, *operands)


def normed_kernel(at_ref, state_ref, c_ref, grow_ref, y_ref, gate_ref, gain_ref, _, out_ref):
    width = y_ref.shape[2]
    heads = grow_ref.shape[3]
    from_state = jnp.dot(c_ref[0, 0], state_ref[0], preferred_element_type=jnp.float32)
    ssd_out = y_ref[0] + from_state * spread(grow_ref[0, 0], width // heads)
    gate = gate_ref[0].astype(jnp.float32)
    gated = ssd_out * (gate / (1.0 + jnp.exp(-gate)))
    scale = lax.rsqrt(jnp.mean(gated * gated, axis=1, keepdims=True) + norm_eps)
    out_ref[0, 0] = (gated * scale * gain_ref[0]).astype(jnp.bfloat16)


def normed_part(index, at, state, c, grow, y, gate, gain, normed):
    sessions, tokens, inner = y.shape
    groups, state_size = c.shape[1], c.shape[3]
    width = inner // groups
    heads = grow.shape[3]
    by_both = lambda s, at: (s, at[0], 0, 0)
    flat = pl.BlockSpec((1, tokens, width), lambda s, at: (s, 0, at[0]))
    return pl.pallas_call(
        normed_kernel,
        grid_spec=pltpu.PrefetchScalarGridSpec(
            num_scalar_prefetch=1,
            grid=(sessions,),
            in_specs=[
                pl.BlockSpec((1, state_size, width), lambda s, at: (s, 0, 0)),
                pl.BlockSpec((1, 1, tokens, state_size), by_both),
                pl.BlockSpec((1, 1, tokens, heads), by_both),
                flat,
                flat,
                pl.BlockSpec((1, 1, width), lambda s, at: (at[0], 0, 0)),
                pl.BlockSpec(memory_space=pl.ANY),
            ],
            out_specs=pl.BlockSpec((1, 1, tokens, width), lambda s, at: (index, s, 0, 0)),
        ),
        out_shape=jax.ShapeDtypeStruct(normed.shape, normed.dtype),
        input_output_aliases={7: 0},
        compiler_params=pltpu.CompilerParams(vmem_limit_bytes=VMEM),
        cost_estimate=pl.CostEstimate(
            flops=10**8, bytes_accessed=4 * 2**20, transcendentals=2**19
        ),
        name="normed_part",
    )(at, state, c, grow, y, gate, gain, normed)


def pick_kernel(slot_ref, pool_ref, out_ref):
    heads, cols, head_dim = pool_ref.shape[1:]
    groups = out_ref.shape[0]
    per = heads // groups
    for g in range(groups):
        held = [pool_ref[0, g * per + h] for h in range(per)]
        out_ref[g, 0] = jnp.concatenate(held, axis=1).astype(jnp.bfloat16)


def pick_part(asked, pool, groups):
    _, heads, cols, head_dim = pool.shape
    count = asked.shape[0]
    width = heads // groups * head_dim
    return pl.pallas_call(
        pick_kernel,
        grid_spec=pltpu.PrefetchScalarGridSpec(
            num_scalar_prefetch=1,
            grid=(count,),
            in_specs=[pl.BlockSpec((1, heads, cols, head_dim), lambda i, slot: (slot[i], 0, 0, 0))],
            out_specs=pl.BlockSpec((groups, 1, cols, width), lambda i, slot: (0, i, 0, 0)),
        ),
        out_shape=jax.ShapeDtypeStruct((groups, count, cols, width), jnp.bfloat16),
        compiler_params=pltpu.CompilerParams(vmem_limit_bytes=VMEM),
        name="pick_part",
    )(asked, pool)


def final_kernel(turn_ref, *refs):
    parts, out_ref = refs[:-1], refs[-1]
    heads, _, head_dim = out_ref.shape[1:]
    value = parts[0][0, 0].astype(jnp.float32)
    for k in range(1, len(parts)):
        value = jnp.where(turn_ref[0] == k, parts[k][0, 0].astype(jnp.float32), value)
    for h in range(heads):
        out_ref[0, h] = value[:, h * head_dim : (h + 1) * head_dim]


def final_part(turn, parts, heads, head_dim):
    groups, sessions, cols, width = parts[0].shape
    per = heads // groups
    return pl.pallas_call(
        final_kernel,
        grid_spec=pltpu.PrefetchScalarGridSpec(
            num_scalar_prefetch=1,
            grid=(sessions, groups),
            in_specs=[pl.BlockSpec((1, 1, cols, width), lambda s, g, _: (g, s, 0, 0)) for _ in parts],
            out_specs=pl.BlockSpec((1, per, cols, head_dim), lambda s, g, _: (s, g, 0, 0)),
        ),
        out_shape=jax.ShapeDtypeStruct((sessions, heads, cols, head_dim), jnp.float32),
        compiler_params=pltpu.CompilerParams(vmem_limit_bytes=VMEM),
        name="final_part",
    )(turn.reshape(1).astype(jnp.int32), *parts)


def local_part(limits, x, b, c, raw, bias, rate, skip):
    sessions, tokens, inner = x.shape
    groups = b.shape[1]
    state = b.shape[3]
    heads = raw.shape[2]
    width = inner // groups

    def by_group(*block):
        return pl.BlockSpec((1, *block), lambda s, g, _: (g, 0, 0))

    def by_both(*block):
        return pl.BlockSpec((1, 1, *block), lambda s, g, _: (s, g, 0, 0))

    def by_turn(*block):
        return pl.BlockSpec((1, 1, *block), lambda s, g, _: (g, s, 0, 0))

    flat = pl.BlockSpec((1, tokens, width), lambda s, g, _: (s, 0, g))
    f32 = jnp.float32
    return pl.pallas_call(
        local_kernel,
        grid_spec=pltpu.PrefetchScalarGridSpec(
            num_scalar_prefetch=1,
            grid=(sessions, groups),
            in_specs=[
                flat,
                by_both(tokens, state),
                by_both(tokens, state),
                by_both(heads, tokens),
                by_group(heads, 1),
                by_group(heads, 1),
                by_group(1, width),
            ],
            out_specs=[
                flat,
                by_turn(state, width),
                by_turn(8, width),
                by_both(tokens, heads),
            ],
        ),
        out_shape=[
            jax.ShapeDtypeStruct((sessions, tokens, inner), f32),
            jax.ShapeDtypeStruct((groups, sessions, state, width), f32),
            jax.ShapeDtypeStruct((groups, sessions, 8, width), f32),
            jax.ShapeDtypeStruct((sessions, groups, tokens, heads), f32),
        ],
        compiler_params=pltpu.CompilerParams(vmem_limit_bytes=VMEM),
        cost_estimate=pl.CostEstimate(
            flops=4 * 10**9, bytes_accessed=14 * 2**20, transcendentals=2**22
        ),
        name="local_part",
    )(
        limits,
        x,
        b,
        c,
        raw,
        bias[:, :, None],
        rate[:, :, None],
        skip,
    )


def product_kernel(layout, parts, base_ref, order_ref, *refs):
    lefts, weights, out_ref, held = refs[:parts], refs[parts:-2], refs[-2], refs[-1]

    @pl.when(pl.program_id(0) == 0)
    def _():
        for k in range(parts):
            held[k] = lefts[k][0]

    total = jnp.zeros(out_ref.shape, jnp.float32)
    for (part, low), weight in zip(layout, weights):
        depth = weight.shape[0]
        left = held[order_ref[part], :, low : low + depth]
        total += jnp.dot(left, weight[...], preferred_element_type=jnp.float32)
    out_ref[...] = total.astype(out_ref.dtype)


def product(base, order, lefts, layout, weights, specs):
    parts = len(lefts)
    tokens, rows = lefts[0][0].shape[1:]
    cols = weights[0].shape[1]
    tile = min(cols, TILE)

    def left_spec(place):
        return pl.BlockSpec((1, tokens, rows), lambda j, base, _: (place(base[0]), 0, 0))

    return pl.pallas_call(
        functools.partial(product_kernel, layout, parts),
        grid_spec=pltpu.PrefetchScalarGridSpec(
            num_scalar_prefetch=2,
            grid=(cols // tile,),
            in_specs=[left_spec(place) for _, place in lefts]
            + [pl.BlockSpec((depth, tile), place) for depth, place in specs],
            out_specs=pl.BlockSpec((tokens, tile), lambda j, *_: (0, j)),
            scratch_shapes=[pltpu.VMEM((parts, tokens, rows), jnp.bfloat16)],
        ),
        out_shape=jax.ShapeDtypeStruct((tokens, cols), jnp.bfloat16),
        compiler_params=pltpu.CompilerParams(vmem_limit_bytes=VMEM),
        cost_estimate=pl.CostEstimate(
            flops=2 * tokens * parts * rows * cols,
            bytes_accessed=2 * (tokens * parts * rows + parts * rows * cols + tokens * cols),
            transcendentals=0,
        ),
        name="product",
    )(base.reshape(1).astype(jnp.int32), order, *[left for left, _ in lefts], *weights)


def row_block(k):
    return lambda j, *_: (k, j)


class Clock:
    def __init__(self):
        self.due = {}

    def send(self, key, value, axis, pairs, due):
        with jax.named_scope("_".join(str(k) for k in key)):
            self.due.setdefault(due, {})[key] = lax.ppermute(value, axis, pairs)

    def done(self, tick):
        return self.due.pop(tick, {})


def shards(
    head_input,
    gate_input,
    state_in_proj,
    state_out_proj,
    step_raw,
    head_step_bias,
    decay_log,
    skip_gain,
    norm_gain,
    out_weight,
    pool_states,
    slot_map,
    span_lengths,
):
    turns = lax.axis_size("ctx")
    turn = lax.axis_index("ctx")
    lanes = lax.axis_size("groups")
    lane = lax.axis_index("groups")
    cores = lax.axis_size("sess")
    core = lax.axis_index("sess")
    head_count = lax.axis_size("head")
    head_index = lax.axis_index("head")
    sessions, tokens, inner = head_input.shape
    heads = step_raw.shape[2]
    head_dim = inner // heads
    slots = pool_states.shape[0]
    state_cols = pool_states.shape[3]
    groups = heads // GROUP_HEADS
    width = inner // groups
    bf16 = jnp.bfloat16

    carriers = lanes * cores
    rows = inner // carriers
    carrier = lane * cores + core
    mine = lax.dynamic_slice_in_dim(out_weight, carrier * rows, rows, 0)
    unit = rows // sum(SPLIT)
    lows = [sum(SPLIT[:p]) * unit for p in range(len(SPLIT))]
    pieces = [mine[low : low + size * unit] for low, size in zip(lows, SPLIT)]

    def slots_of(which):
        return lax.dynamic_slice_in_dim(slot_map, which * sessions, sessions)

    own_slots = slots_of(core)
    asked = jnp.concatenate([slots_of((core - by) % cores) for by in range(cores)])
    picked = pick_part(asked % slots, pool_states.transpose(0, 1, 3, 2), groups)
    start = picked[:, :sessions]
    for by in range(1, cores):
        found = picked[:, by * sessions : (by + 1) * sessions]
        found = lax.ppermute(found, "sess", [(i, (i - by) % cores) for i in range(cores)])
        here = (own_slots // slots == (core + by) % cores)[None, :, None, None]
        start = jnp.where(here, found, start)

    first_session = core * sessions
    own_lengths = lax.dynamic_slice_in_dim(span_lengths, first_session, sessions)
    limits = jnp.clip(own_lengths * SPAN - turn * tokens, 0, tokens)
    first_group = head_index * groups

    def grouped(proj):
        return lax.dynamic_slice_in_dim(proj, first_group, groups, 2).swapaxes(1, 2)

    b = grouped(state_in_proj)
    c = grouped(state_out_proj)
    raw = step_raw.swapaxes(1, 2).reshape(sessions, groups, GROUP_HEADS, tokens)
    skip = jnp.repeat(skip_gain, head_dim).reshape(groups, 1, width)
    gain = norm_gain.reshape(groups, 1, width)

    waves = groups + turns - 2
    first_wave = 2
    clock = Clock()
    hops = range(1, turns - 1)
    count = len(SPLIT)
    starts = {}

    def plan(tick, *what):
        starts.setdefault(tick, []).append(what)

    up_due, down_due = {}, {}
    for hop in hops:
        pairs_up = [(i, i + 1) for i in range(hop - 1, turns - 1)]
        pairs_down = [(i + 1, i) for i in range(turns - hop)]
        for p in range(count):
            if hop == 1:
                at, due = ((0, 1), (1, 2))[p]
            else:
                at, due = ((2, 3), (5, 7))[p]
                at, due = at + 3 * (hop - 2), due + 3 * (hop - 2)
            up_due[hop, p] = due
            plan(at, ("up", hop, p), ("up", hop - 1, p), "ctx", pairs_up, due)
            if hop == 1:
                at, due = ((2, 3), (3, 4))[p]
            else:
                at, due = ((4, 5), (5, 6))[p]
                at, due = at + 3 * (hop - 2), due + 3 * (hop - 2)
            down_due[hop, p] = due
            plan(at, ("down", hop, p), ("down", hop - 1, p), "ctx", pairs_down, due)
    ready = {}
    for j in range(1, turns):
        holders = range(turns)
        for p in range(count):
            if j == 1:
                holders = range(turns - 1)
                at, due = ((4, 5), (5, 6))[p]
            elif j == turns - 1:
                holders = range(1, turns)
                at, due = ((2, 3), (3, 4))[p]
            else:
                at = max(down_due[j, p], up_due[turns - j, p]) + 1
                due = at + 1
            for by_lane in range(1, lanes):
                pairs = [
                    (y * turns + z, (y - by_lane) % lanes * turns + z)
                    for y in range(lanes)
                    for z in holders
                ]
                plan(at, ("part", j, p, by_lane, 0), ("part", j, p, 0, 0), ("groups", "ctx"), pairs, due)
            for by_lane in range(lanes):
                for by in range(1, cores):
                    pairs = [
                        (z * cores + k, z * cores + (k - by) % cores)
                        for z in holders
                        for k in range(cores)
                    ]
                    plan(
                        due + 1,
                        ("part", j, p, by_lane, by),
                        ("part", j, p, by_lane, 0),
                        ("ctx", "sess"),
                        pairs,
                        due + 1,
                    )
            ready[j, p] = due + 1
    half = max(1, groups // 2)
    begun = [range(0, half), range(half, groups)]
    for k, part in enumerate(begun):
        for other in range(1, turns):
            if len(part):
                plan(1 + k, ("first", k, other), ("start", k), "ctx", [(other, 0)], 1 + 2 * k)
    last_tick = max(max(starts), first_wave + waves) + 1

    have = {}
    for p in range(count):
        have["up", 0, p] = have["down", 0, p] = pieces[p]
    for k, part in enumerate(begun):
        have["start", k] = start[part.start : part.stop]

    def resolve(key):
        if key in have:
            return have[key]
        if key[0] == "part" and key[3:] == (0, 0):
            _, j, p = key[:3]
            if j == 1:
                have[key] = have["down", 1, p]
            elif j == turns - 1:
                have[key] = have["up", 1, p]
            else:
                have[key] = jnp.where(turn + j < turns, have["down", j, p], have["up", turns - j, p])
        return have[key]

    normed = jnp.zeros((waves + 1, sessions, tokens, width), bf16)
    leavings, lent = [], []
    y = end = keep = grow = None
    batches = [(0, groups)] if groups < 3 else [(0, 2)] + [(g, g + 1) for g in range(2, groups)]
    for tick in range(last_tick + 1):
        sends = starts.get(tick, [])
        values = clock.done(tick - 1)
        have.update(values)
        for key, source, axis, pairs, due in sends:
            values[source] = resolve(source)
        if tick == 1:
            values["x"] = head_input
        if tick == 2:
            values.update(y=y, end=end, keep=keep, grow=grow)
        have.update(zip(values, lax.optimization_barrier(tuple(values.values()))))
        if tick == 2:
            y, end, keep, grow = (have[k] for k in ("y", "end", "keep", "grow"))
        index = tick - first_wave
        if 0 <= index <= waves:
            at = jnp.clip(index - turn, 0, groups - 1)
            coming = have["wave", index - 1] if index else None
            first, inside = None, 0
            if index < groups:
                k = 0 if index < half else 1
                inside = index - begun[k].start
                first = [have["start", k]] + [have["first", k, other] for other in range(1, turns)]
            at = jnp.stack([at, turn]).astype(jnp.int32)
            state, leaving = leave_part(at, coming, first, inside, keep, end)
            leavings.append(leaving)
            if index < waves:
                pairs = [(i, i + 1) for i in range(turns - 1) if 0 <= index - i < groups]
                clock.send(("wave", index), leaving, "ctx", pairs, tick)
        for key, source, axis, pairs, due in sends:
            clock.send(key, have[source], axis, pairs, due)
        if tick == 1:
            y, end, keep, grow = local_part(
                limits,
                have["x"],
                b,
                c,
                raw,
                head_step_bias.reshape(groups, GROUP_HEADS),
                decay_log.reshape(groups, GROUP_HEADS),
                skip,
            )
        if 0 <= index <= waves:
            normed = normed_part(index, at, state, c, grow, y, gate_input, gain, normed)
        for low, high in batches:
            if index == turns - 2 + high:
                chunk = lax.dynamic_slice_in_dim(
                    normed, jnp.where(turn == 0, 0, turns - 1) + low, high - low, 0
                )
                chunk = chunk.reshape(high - low, sessions * tokens, width)
                clock.send(
                    ("inward", low),
                    chunk,
                    "ctx",
                    [(0, 1), (turns - 1, turns - 2)],
                    min(tick + 1, last_tick),
                )
    for late in sorted(clock.due):
        have.update(clock.due[late])

    ended = []
    for to in range(turns):
        cut = [leavings[turns - 1 + g][:, to * state_cols : (to + 1) * state_cols] for g in range(groups)]
        ended.append(jnp.stack(cut))
    tied = lax.optimization_barrier((*ended, have["inward", batches[-1][0]]))
    ended, have["inward", batches[-1][0]] = list(tied[:-1]), tied[-1]
    for to in range(turns - 1):
        ended[to] = lax.ppermute(ended[to], "ctx", [(turns - 1, to)])
    final_states = final_part(turn, ended, heads, head_dim).transpose(0, 1, 3, 2)

    def as_left(held):
        held = held.transpose(1, 0, 2).reshape(sessions * tokens, carriers, rows)
        return held.transpose(1, 0, 2)

    def at_place(k):
        return lambda base: base + k

    def at_fixed(k):
        return lambda base: k

    base = turn
    if groups == carriers:
        held = normed.reshape(waves + 1, sessions * tokens, width)
        left = [(held, at_place(k)) for k in range(carriers)]
        lent = [
            (have["inward", low], at_fixed(k)) for low, high in batches for k in range(high - low)
        ]
    else:
        held = lax.dynamic_slice_in_dim(normed, turn, groups, 0)
        held = as_left(held.reshape(groups, sessions * tokens, width))
        left = [(held, at_fixed(k)) for k in range(carriers)]
        held = jnp.concatenate([have["inward", low] for low, _ in batches], axis=0)
        held = as_left(held)
        lent = [(held, at_fixed(k)) for k in range(carriers)]
    order = jnp.stack(
        [
            (lane + by_lane) % lanes * cores + (core + by) % cores
            for by_lane in range(lanes)
            for by in range(cores)
        ]
    ).astype(jnp.int32)
    layout, specs = [], []
    for k in range(carriers):
        for p in range(count):
            layout.append((k, lows[p]))
            specs.append((SPLIT[p] * unit, row_block(0)))

    def parts_of(j):
        return [
            resolve(("part", j, p, by_lane, by))
            for by_lane in range(lanes)
            for by in range(cores)
            for p in range(count)
        ]

    blocks = {}
    blocks[0] = product(
        base,
        jnp.arange(carriers, dtype=jnp.int32),
        left,
        [(k, 0) for k in range(carriers)],
        [out_weight] * carriers,
        [(rows, row_block(k)) for k in range(carriers)],
    )
    for j in [1, turns - 1] + list(range(2, turns - 1)):
        blocks[j] = product(base, order, left, layout, parts_of(j), specs)
    if turns == 4:
        far_block = product(base, order, lent, layout, parts_of(2), specs)
    else:
        far_block = jnp.where(
            turn == 1,
            product(base, order, lent, layout, parts_of(turns - 2), specs),
            product(base, order, lent, layout, parts_of(2), specs),
        )
    live = (jnp.arange(tokens, dtype=jnp.int32)[None, :] < limits[:, None]).astype(jnp.float32)
    if head_count == 2:
        share = turns // 2

        def across(j, skipped):
            pairs = []
            for z in range(turns):
                to = (z + j) % turns // share
                if z not in skipped:
                    pairs.append((z * 2 + 1 - to, z * 2 + to))
            return lax.ppermute(blocks[j], ("ctx", "head"), pairs)

        skipped = {1: (turns - 1,), turns - 1: (0,)}
        other = {j: across(j, skipped.get(j, ())) for j in blocks}
        same = lax.ppermute(
            far_block, ("ctx", "head"), [(1 * 2 + 1, 0 * 2 + 1), ((turns - 2) * 2, (turns - 1) * 2)]
        )
        cross = lax.ppermute(
            far_block, ("ctx", "head"), [(1 * 2, 0 * 2 + 1), ((turns - 2) * 2 + 1, (turns - 1) * 2)]
        )
        sums = []
        for m in range(share):
            wanted = (head_index * share + m - turn) % turns
            ends = ((turn == 0) & (wanted == turns - 1)) | ((turn == turns - 1) & (wanted == 1))
            mine_now, theirs = same, cross
            for j in blocks:
                chosen = (wanted == j) & ~ends
                mine_now = jnp.where(chosen, blocks[j], mine_now)
                theirs = jnp.where(chosen, other[j], theirs)
            sums.append(mine_now.astype(jnp.float32) + theirs.astype(jnp.float32))
        summed = jnp.concatenate(sums, axis=1).reshape(sessions, tokens, -1)
    else:
        back = lax.ppermute(far_block, "ctx", [(1, 0), (turns - 2, turns - 1)])
        blocks[1] = jnp.where(turn == turns - 1, back, blocks[1])
        blocks[turns - 1] = jnp.where(turn == 0, back, blocks[turns - 1])
        stacked = jnp.stack([blocks[j] for j in range(turns)])
        stacked = lax.dynamic_slice_in_dim(
            jnp.concatenate([stacked, stacked], axis=0), (turns - turn) % turns, turns, 0
        )
        partial = stacked.transpose(1, 0, 2).reshape(sessions, tokens, -1)
        summed = lax.psum_scatter(partial, "head", scatter_dimension=2, tiled=True).astype(
            jnp.float32
        )
    mixed = (summed * live[:, :, None]).astype(bf16)
    return (mixed, final_states)


def solution(mesh):
    placed = (
        P(("groups", "sess"), "ctx", "head"),
        P(("groups", "sess"), "ctx", "head"),
        P(("groups", "sess"), "ctx", None, None),
        P(("groups", "sess"), "ctx", None, None),
        P(("groups", "sess"), "ctx", "head"),
        P("head"),
        P("head"),
        P("head"),
        P("head"),
        P("head", "ctx"),
        P(("groups", "sess"), "head", None, "ctx"),
        P("groups"),
        P("groups"),
    )
    return jax.shard_map(
        shards,
        mesh=mesh,
        in_specs=placed,
        out_specs=(
            P(("groups", "sess"), "ctx", "head"),
            P(("groups", "sess"), "head", None, "ctx"),
        ),
        check_vma=False,
    )
```

```python
import functools

import jax
import jax.numpy as jnp
from jax import lax
from jax.experimental import pallas as pl
from jax.experimental.pallas import tpu as pltpu
from jax.sharding import PartitionSpec as P

HEADS = 128
GROUPS = 8
SPAN = 128
GROUP_HEADS = HEADS // GROUPS
TILE = 512
VMEM = 20 * 1024 * 1024

norm_eps = 1e-05
far = -1e30


def spread(values, head_dim):
    heads = values.shape[1]
    high = values.astype(jnp.bfloat16)
    low = (values - high.astype(jnp.float32)).astype(jnp.bfloat16)
    both = jnp.concatenate([high, low], axis=1)
    row = lax.broadcasted_iota(jnp.int32, (2 * heads, heads * head_dim), 0)
    col = lax.broadcasted_iota(jnp.int32, (2 * heads, heads * head_dim), 1)
    ones = (col // head_dim == row % heads).astype(jnp.bfloat16)
    return jnp.dot(both, ones, preferred_element_type=jnp.float32)


def decays(limit_ref, raw_ref, bias_ref, rate_ref):
    heads, tokens = raw_ref.shape[2:]
    f32 = jnp.float32
    token = lax.broadcasted_iota(jnp.int32, (heads, tokens), 1)
    size = jax.nn.softplus(raw_ref[0, 0] + bias_ref[0])
    size = size * (token < limit_ref[pl.program_id(0)]).astype(f32)
    log_keep = -jnp.exp(rate_ref[0]) * size
    row = lax.broadcasted_iota(jnp.int32, (tokens, tokens), 0)
    col = lax.broadcasted_iota(jnp.int32, (tokens, tokens), 1)
    cum = jnp.dot(log_keep, (row <= col).astype(f32), precision=lax.Precision.HIGHEST)
    return size, cum, row >= col


def end_kernel(
    limit_ref, x_ref, b_ref, raw_ref, bias_ref, rate_ref, end_ref, keep_ref, grow_ref
):
    tokens, width = x_ref.shape[1:]
    heads = raw_ref.shape[2]
    head_dim = width // heads
    f32 = jnp.float32
    size, cum, _ = decays(limit_ref, raw_ref, bias_ref, rate_ref)
    last = cum[:, tokens - 1 : tokens]
    tail = spread((jnp.exp(last - cum) * size).T, head_dim)
    weighted = (tail * x_ref[0].astype(f32)).astype(jnp.bfloat16)
    b_t = b_ref[0, 0].astype(f32).T.astype(jnp.bfloat16)
    end_ref[0, 0] = jnp.dot(b_t, weighted, preferred_element_type=f32)
    grow = jnp.exp(cum.T)
    keep_ref[0, 0] = spread(jnp.broadcast_to(grow[tokens - 1 :], (8, heads)), head_dim)
    grow_ref[0, 0] = grow


def inside_kernel(
    limit_ref, x_ref, b_ref, c_ref, raw_ref, bias_ref, rate_ref, skip_ref, y_ref
):
    tokens, width = x_ref.shape[1:]
    heads = raw_ref.shape[2]
    head_dim = width // heads
    f32 = jnp.float32
    size, cum, causal = decays(limit_ref, raw_ref, bias_ref, rate_ref)
    cum_t = cum.T
    shifted = cum - jnp.where(size > 0, jnp.log(jnp.where(size > 0, size, 1.0)), far)
    scores = lax.dot_general(
        c_ref[0, 0], b_ref[0, 0], (((1,), (1,)), ((), ())), preferred_element_type=f32
    )
    lane = lax.broadcasted_iota(jnp.int32, (tokens, 2 * head_dim), 1)
    for pair in range(heads // 2):
        decayed = []
        for head in (2 * pair, 2 * pair + 1):
            gap = cum_t[:, head : head + 1] - shifted[head : head + 1, :]
            decayed.append((scores * jnp.exp(jnp.where(causal, gap, far))).astype(jnp.bfloat16))
        here = pl.ds(pair * 2 * head_dim, 2 * head_dim)
        x = x_ref[0, :, here]
        zero = jnp.zeros_like(x)
        apart = jnp.concatenate(
            [jnp.where(lane < head_dim, x, zero), jnp.where(lane >= head_dim, x, zero)], axis=0
        )
        y = jnp.dot(jnp.concatenate(decayed, axis=1), apart, preferred_element_type=f32)
        y_ref[0, :, here] = y + skip_ref[0, :, here] * x.astype(f32)


def local_specs(x, b, raw):
    tokens, width = x.shape[1], x.shape[2] // b.shape[1]
    state, heads = b.shape[3], raw.shape[2]

    def by_group(*block):
        return pl.BlockSpec((1, *block), lambda s, g, _: (g, 0, 0))

    def by_both(*block):
        return pl.BlockSpec((1, 1, *block), lambda s, g, _: (s, g, 0, 0))

    flat = pl.BlockSpec((1, tokens, width), lambda s, g, _: (s, 0, g))
    return (
        flat,
        by_both(tokens, state),
        by_both(heads, tokens),
        by_group(heads, 1),
        by_group(1, width),
    )


def end_part(limits, x, b, raw, bias, rate):
    sessions, tokens, inner = x.shape
    groups, state, heads = b.shape[1], b.shape[3], raw.shape[2]
    width = inner // groups
    flat, proj, per_token, per_head, _ = local_specs(x, b, raw)
    f32 = jnp.float32
    by_turn = lambda s, g, _: (g, s, 0, 0)
    return pl.pallas_call(
        end_kernel,
        grid_spec=pltpu.PrefetchScalarGridSpec(
            num_scalar_prefetch=1,
            grid=(sessions, groups),
            in_specs=[flat, proj, per_token, per_head, per_head],
            out_specs=[
                pl.BlockSpec((1, 1, state, width), by_turn),
                pl.BlockSpec((1, 1, 8, width), by_turn),
                pl.BlockSpec((1, 1, tokens, heads), lambda s, g, _: (s, g, 0, 0)),
            ],
        ),
        out_shape=[
            jax.ShapeDtypeStruct((groups, sessions, state, width), f32),
            jax.ShapeDtypeStruct((groups, sessions, 8, width), f32),
            jax.ShapeDtypeStruct((sessions, groups, tokens, heads), f32),
        ],
        compiler_params=pltpu.CompilerParams(vmem_limit_bytes=VMEM),
        cost_estimate=pl.CostEstimate(
            flops=2 * 10**9, bytes_accessed=8 * 2**20, transcendentals=2**18
        ),
        name="end_part",
    )(limits, x, b, raw, bias[:, :, None], rate[:, :, None])


def inside_part(limits, x, b, c, raw, bias, rate, skip):
    sessions, tokens, inner = x.shape
    groups = b.shape[1]
    flat, proj, per_token, per_head, per_channel = local_specs(x, b, raw)
    return pl.pallas_call(
        inside_kernel,
        grid_spec=pltpu.PrefetchScalarGridSpec(
            num_scalar_prefetch=1,
            grid=(sessions, groups),
            in_specs=[flat, proj, proj, per_token, per_head, per_head, per_channel],
            out_specs=flat,
        ),
        out_shape=jax.ShapeDtypeStruct((sessions, tokens, inner), jnp.float32),
        compiler_params=pltpu.CompilerParams(vmem_limit_bytes=VMEM),
        cost_estimate=pl.CostEstimate(
            flops=4 * 10**9, bytes_accessed=8 * 2**20, transcendentals=2**22
        ),
        name="inside_part",
    )(limits, x, b, c, raw, bias[:, :, None], rate[:, :, None], skip)


def leave_kernel(count, kind, *refs):
    at_ref, refs = refs[0], refs[1:]
    keep_ref, end_ref, state_ref, leaving_ref = refs[-4:]
    state = None
    if kind != "only":
        state = refs[0][0].astype(jnp.float32)
        refs = refs[1:]
    if count:
        first = jnp.concatenate([r[0, 0].astype(jnp.float32) for r in refs[:count]], axis=0)
        state = first if state is None else jnp.where(at_ref[1] == 0, first, state)
    state_ref[0] = state.astype(jnp.bfloat16)
    leaving_ref[0] = (keep_ref[0, 0, :1] * state + end_ref[0, 0]).astype(jnp.bfloat16)


def leave_part(at, coming, first, inside, keep, end):
    groups, sessions, state_size, width = end.shape
    by_turn = lambda s, at: (at[0], s, 0, 0)
    whole = pl.BlockSpec((1, state_size, width), lambda s, at: (s, 0, 0))
    operands, specs = [], []
    if coming is not None:
        operands.append(coming)
        specs.append(whole)
    if first is not None:
        operands += first
        specs += [
            pl.BlockSpec((1, 1, *f.shape[2:]), lambda s, at: (inside, s, 0, 0)) for f in first
        ]
    operands += [keep, end]
    specs += [
        pl.BlockSpec((1, 1, *keep.shape[2:]), by_turn),
        pl.BlockSpec((1, 1, state_size, width), by_turn),
    ]
    kind = None if first is None else ("only" if coming is None else "both")
    shape = jax.ShapeDtypeStruct((sessions, state_size, width), jnp.bfloat16)
    return pl.pallas_call(
        functools.partial(leave_kernel, 0 if first is None else len(first), kind),
        grid_spec=pltpu.PrefetchScalarGridSpec(
            num_scalar_prefetch=1, grid=(sessions,), in_specs=specs, out_specs=[whole, whole]
        ),
        out_shape=[shape, shape],
        compiler_params=pltpu.CompilerParams(vmem_limit_bytes=VMEM),
        cost_estimate=pl.CostEstimate(flops=10**6, bytes_accessed=3 * 2**20, transcendentals=0),
        name="leave_part",
    )(at, *operands)


def normed_kernel(at_ref, state_ref, c_ref, grow_ref, y_ref, gate_ref, gain_ref, _, out_ref):
    width = y_ref.shape[2]
    heads = grow_ref.shape[3]
    from_state = jnp.dot(c_ref[0, 0], state_ref[0], preferred_element_type=jnp.float32)
    ssd_out = y_ref[0] + from_state * spread(grow_ref[0, 0], width // heads)
    gate = gate_ref[0].astype(jnp.float32)
    gated = ssd_out * (gate / (1.0 + jnp.exp(-gate)))
    scale = lax.rsqrt(jnp.mean(gated * gated, axis=1, keepdims=True) + norm_eps)
    out_ref[0, 0] = (gated * scale * gain_ref[0]).astype(jnp.bfloat16)


def normed_part(index, at, state, c, grow, y, gate, gain, normed):
    sessions, tokens, inner = y.shape
    groups, state_size = c.shape[1], c.shape[3]
    width = inner // groups
    heads = grow.shape[3]
    by_both = lambda s, at: (s, at[0], 0, 0)
    flat = pl.BlockSpec((1, tokens, width), lambda s, at: (s, 0, at[0]))
    return pl.pallas_call(
        normed_kernel,
        grid_spec=pltpu.PrefetchScalarGridSpec(
            num_scalar_prefetch=1,
            grid=(sessions,),
            in_specs=[
                pl.BlockSpec((1, state_size, width), lambda s, at: (s, 0, 0)),
                pl.BlockSpec((1, 1, tokens, state_size), by_both),
                pl.BlockSpec((1, 1, tokens, heads), by_both),
                flat,
                flat,
                pl.BlockSpec((1, 1, width), lambda s, at: (at[0], 0, 0)),
                pl.BlockSpec(memory_space=pl.ANY),
            ],
            out_specs=pl.BlockSpec((1, 1, tokens, width), lambda s, at: (index, s, 0, 0)),
        ),
        out_shape=jax.ShapeDtypeStruct(normed.shape, normed.dtype),
        input_output_aliases={7: 0},
        compiler_params=pltpu.CompilerParams(vmem_limit_bytes=VMEM),
        cost_estimate=pl.CostEstimate(
            flops=10**8, bytes_accessed=4 * 2**20, transcendentals=2**19
        ),
        name="normed_part",
    )(at, state, c, grow, y, gate, gain, normed)


def pick_kernel(slot_ref, pool_ref, out_ref):
    heads, cols, head_dim = pool_ref.shape[1:]
    groups = out_ref.shape[0]
    per = heads // groups
    for g in range(groups):
        held = [pool_ref[0, g * per + h] for h in range(per)]
        out_ref[g, 0] = jnp.concatenate(held, axis=1).astype(jnp.bfloat16)


def pick_part(asked, pool, groups):
    _, heads, cols, head_dim = pool.shape
    count = asked.shape[0]
    width = heads // groups * head_dim
    return pl.pallas_call(
        pick_kernel,
        grid_spec=pltpu.PrefetchScalarGridSpec(
            num_scalar_prefetch=1,
            grid=(count,),
            in_specs=[pl.BlockSpec((1, heads, cols, head_dim), lambda i, slot: (slot[i], 0, 0, 0))],
            out_specs=pl.BlockSpec((groups, 1, cols, width), lambda i, slot: (0, i, 0, 0)),
        ),
        out_shape=jax.ShapeDtypeStruct((groups, count, cols, width), jnp.bfloat16),
        compiler_params=pltpu.CompilerParams(vmem_limit_bytes=VMEM),
        name="pick_part",
    )(asked, pool)


def final_kernel(value_ref, out_ref):
    heads, _, head_dim = out_ref.shape[1:]
    value = value_ref[0, 0].astype(jnp.float32)
    for h in range(heads):
        out_ref[0, h] = value[:, h * head_dim : (h + 1) * head_dim]


def final_part(value, heads, head_dim):
    groups, sessions, cols, width = value.shape
    per = heads // groups
    return pl.pallas_call(
        final_kernel,
        grid=(sessions, groups),
        in_specs=[pl.BlockSpec((1, 1, cols, width), lambda s, g: (g, s, 0, 0))],
        out_specs=pl.BlockSpec((1, per, cols, head_dim), lambda s, g: (s, g, 0, 0)),
        out_shape=jax.ShapeDtypeStruct((sessions, heads, cols, head_dim), jnp.float32),
        compiler_params=pltpu.CompilerParams(vmem_limit_bytes=VMEM),
        name="final_part",
    )(value)


def product_kernel(parts, base_ref, block_ref, *refs):
    lefts, weights, out_ref, held = refs[:parts], refs[parts:-2], refs[-2], refs[-1]

    @pl.when((pl.program_id(0) == 0) & (pl.program_id(1) == 0))
    def _():
        for k in range(parts):
            held[k] = lefts[k][0]

    total = jnp.zeros(out_ref.shape, jnp.float32)
    for k in range(parts):
        total += jnp.dot(held[k], weights[k][...], preferred_element_type=jnp.float32)
    out_ref[...] = total.astype(out_ref.dtype)


def product(base, blocks, lefts, gathered, row_at):
    parts = len(lefts)
    tokens, rows = lefts[0][0].shape[1:]
    count = blocks.shape[0]
    cols = gathered.shape[1]
    tile = min(cols, TILE)
    tiles = cols // tile

    def left_spec(place):
        return pl.BlockSpec((1, tokens, rows), lambda i, j, base, _: (place(base[0]), 0, 0))

    def weight_spec(k):
        return pl.BlockSpec((rows, tile), lambda i, j, _, blocks: (row_at(k, blocks[i]), j))

    return pl.pallas_call(
        functools.partial(product_kernel, parts),
        grid_spec=pltpu.PrefetchScalarGridSpec(
            num_scalar_prefetch=2,
            grid=(count, tiles),
            in_specs=[left_spec(place) for _, place in lefts]
            + [weight_spec(k) for k in range(parts)],
            out_specs=pl.BlockSpec((tokens, tile), lambda i, j, *_: (0, i * tiles + j)),
            scratch_shapes=[pltpu.VMEM((parts, tokens, rows), jnp.bfloat16)],
        ),
        out_shape=jax.ShapeDtypeStruct((tokens, count * cols), jnp.bfloat16),
        compiler_params=pltpu.CompilerParams(vmem_limit_bytes=VMEM),
        cost_estimate=pl.CostEstimate(
            flops=2 * tokens * parts * rows * cols * count,
            bytes_accessed=2 * (tokens * parts * rows + parts * rows * cols * count),
            transcendentals=0,
        ),
        name="product",
    )(
        base.reshape(1).astype(jnp.int32),
        blocks.astype(jnp.int32),
        *[left for left, _ in lefts],
        *[gathered] * parts,
    )


def shards(
    head_input,
    gate_input,
    state_in_proj,
    state_out_proj,
    step_raw,
    head_step_bias,
    decay_log,
    skip_gain,
    norm_gain,
    out_weight,
    pool_states,
    slot_map,
    span_lengths,
):
    turns = lax.axis_size("ctx")
    turn = lax.axis_index("ctx")
    lanes = lax.axis_size("groups")
    lane = lax.axis_index("groups")
    cores = lax.axis_size("sess")
    core = lax.axis_index("sess")
    head_count = lax.axis_size("head")
    head_index = lax.axis_index("head")
    sessions, tokens, inner = head_input.shape
    heads = step_raw.shape[2]
    head_dim = inner // heads
    slots = pool_states.shape[0]
    state_cols = pool_states.shape[3]
    groups = heads // GROUP_HEADS
    width = inner // groups
    bf16 = jnp.bfloat16

    carriers = lanes * cores
    rows = inner // carriers
    mine = lax.dynamic_slice_in_dim(out_weight, (lane * cores + core) * rows, rows, 0)
    gathered = lax.all_gather(mine, ("groups", "ctx", "sess"), axis=0, tiled=True)

    def row_at(k, q):
        return (k // cores * turns + q) * cores + k % cores

    def slots_of(which):
        return lax.dynamic_slice_in_dim(slot_map, which * sessions, sessions)

    own_slots = slots_of(core)
    asked = jnp.concatenate([slots_of((core - by) % cores) for by in range(cores)])
    picked = pick_part(asked % slots, pool_states.transpose(0, 1, 3, 2), groups)
    start = picked[:, :sessions]
    for by in range(1, cores):
        found = picked[:, by * sessions : (by + 1) * sessions]
        found = lax.ppermute(found, "sess", [(i, (i - by) % cores) for i in range(cores)])
        here = (own_slots // slots == (core + by) % cores)[None, :, None, None]
        start = jnp.where(here, found, start)
    entering = []
    for g in range(groups):
        part = start[g : g + 1]
        if g:
            part, entering[-1] = lax.optimization_barrier((part, entering[-1]))
        entering.append([part] + [lax.ppermute(part, "ctx", [(k, 0)]) for k in range(1, turns)])

    first_session = core * sessions
    own_lengths = lax.dynamic_slice_in_dim(span_lengths, first_session, sessions)
    limits = jnp.clip(own_lengths * SPAN - turn * tokens, 0, tokens)
    first_group = head_index * groups

    def grouped(proj):
        return lax.dynamic_slice_in_dim(proj, first_group, groups, 2).swapaxes(1, 2)

    b = grouped(state_in_proj)
    c = grouped(state_out_proj)
    raw = step_raw.swapaxes(1, 2).reshape(sessions, groups, GROUP_HEADS, tokens)
    skip = jnp.repeat(skip_gain, head_dim).reshape(groups, 1, width)
    gain = norm_gain.reshape(groups, 1, width)
    bias = head_step_bias.reshape(groups, GROUP_HEADS)
    rate = decay_log.reshape(groups, GROUP_HEADS)
    end, keep, grow = end_part(limits, head_input, b, raw, bias, rate)

    waves = groups + turns - 2
    normed = jnp.zeros((waves + 1, sessions, tokens, width), bf16)
    leavings = []
    coming = None
    for index in range(waves + 1):
        at = jnp.stack([jnp.clip(index - turn, 0, groups - 1), turn]).astype(jnp.int32)
        given = entering[index] if index < groups else None
        state, leaving = leave_part(at, coming, given, 0, keep, end)
        leavings.append(leaving)
        if index < waves:
            pairs = [(i, i + 1) for i in range(turns - 1) if 0 <= index - i < groups]
            coming = lax.ppermute(leaving, "ctx", pairs)
        if index == 0:
            x, state = lax.optimization_barrier((head_input, state))
            y = inside_part(limits, x, b, c, raw, bias, rate, skip)
        normed = normed_part(index, at, state, c, grow, y, gate_input, gain, normed)
        if index < waves:
            coming, normed = lax.optimization_barrier((coming, normed))

    final = jnp.stack(leavings[turns - 1 :])
    for step in range((turns - 1).bit_length()):
        by = turns // 2 ** (step + 1)
        half = final.shape[2] // 2
        pairs = [(z, z - by) for z in range(turns) if (turns - 1 - z) % (2 * by) == 0]
        got = lax.ppermute(final[:, :, :half], "ctx", pairs)
        final = jnp.where((turns - 1 - turn) % (2 * by) == by, got, final[:, :, half:])
    final = final_part(final, heads, head_dim)

    def at_place(k):
        return lambda base: base + k

    def at_fixed(k):
        return lambda base: k

    if groups == carriers:
        held = normed.reshape(waves + 1, sessions * tokens, width)
        left = [(held, at_place(k)) for k in range(carriers)]
    else:
        held = lax.dynamic_slice_in_dim(normed, turn, groups, 0)
        held = held.reshape(groups, sessions * tokens, width)
        held = held.transpose(1, 0, 2).reshape(sessions * tokens, carriers, rows)
        held = held.transpose(1, 0, 2)
        left = [(held, at_fixed(k)) for k in range(carriers)]
    live = (jnp.arange(tokens, dtype=jnp.int32)[None, :] < limits[:, None]).astype(jnp.float32)
    if head_count == 2:
        share = turns // 2
        theirs = []
        for m in range(share):
            block = product(turn, ((1 - head_index) * share + m).reshape(1), left, gathered, row_at)
            theirs.append(lax.ppermute(block, "head", [(0, 1), (1, 0)]))
        ours = product(turn, head_index * share + jnp.arange(share), left, gathered, row_at)
        theirs, ours, final = lax.optimization_barrier((theirs, ours, final))
        summed = ours.astype(jnp.float32) + jnp.concatenate(theirs, axis=1).astype(jnp.float32)
        summed = summed.reshape(sessions, tokens, -1)
    else:
        partial = product(turn, jnp.arange(turns), left, gathered, row_at)
        partial = partial.reshape(sessions, tokens, -1)
        summed = lax.psum_scatter(partial, "head", scatter_dimension=2, tiled=True).astype(
            jnp.float32
        )
    mixed = (summed * live[:, :, None]).astype(bf16)
    return (mixed, final.transpose(0, 1, 3, 2))


def solution(mesh):
    placed = (
        P(("groups", "sess"), "ctx", "head"),
        P(("groups", "sess"), "ctx", "head"),
        P(("groups", "sess"), "ctx", None, None),
        P(("groups", "sess"), "ctx", None, None),
        P(("groups", "sess"), "ctx", "head"),
        P("head"),
        P("head"),
        P("head"),
        P("head"),
        P("head", "ctx"),
        P(("groups", "sess"), "head", None, "ctx"),
        P("groups"),
        P("groups"),
    )
    return jax.shard_map(
        shards,
        mesh=mesh,
        in_specs=placed,
        out_specs=(
            P(("groups", "sess"), "ctx", "head"),
            P(("groups", "sess"), "head", None, "ctx"),
        ),
        check_vma=False,
    )
```

```python
import functools

import jax
import jax.numpy as jnp
from jax import lax
from jax.experimental import pallas as pl
from jax.experimental.pallas import tpu as pltpu
from jax.sharding import PartitionSpec as P

HEADS = 128
GROUPS = 8
SPAN = 128
GROUP_HEADS = HEADS // GROUPS
TILE = 512
VMEM = 20 * 1024 * 1024

norm_eps = 1e-05
far = -1e30


def spread(values, head_dim):
    heads = values.shape[1]
    high = values.astype(jnp.bfloat16)
    low = (values - high.astype(jnp.float32)).astype(jnp.bfloat16)
    both = jnp.concatenate([high, low], axis=1)
    row = lax.broadcasted_iota(jnp.int32, (2 * heads, heads * head_dim), 0)
    col = lax.broadcasted_iota(jnp.int32, (2 * heads, heads * head_dim), 1)
    ones = (col // head_dim == row % heads).astype(jnp.bfloat16)
    return jnp.dot(both, ones, preferred_element_type=jnp.float32)


def decays(limit_ref, raw_ref, bias_ref, rate_ref):
    heads, tokens = raw_ref.shape[2:]
    f32 = jnp.float32
    token = lax.broadcasted_iota(jnp.int32, (heads, tokens), 1)
    size = jax.nn.softplus(raw_ref[0, 0] + bias_ref[0])
    size = size * (token < limit_ref[pl.program_id(0)]).astype(f32)
    log_keep = -jnp.exp(rate_ref[0]) * size
    row = lax.broadcasted_iota(jnp.int32, (tokens, tokens), 0)
    col = lax.broadcasted_iota(jnp.int32, (tokens, tokens), 1)
    cum = jnp.dot(log_keep, (row <= col).astype(f32), precision=lax.Precision.HIGHEST)
    return size, cum, row >= col


def end_kernel(
    limit_ref, x_ref, b_ref, raw_ref, bias_ref, rate_ref, end_ref, keep_ref, grow_ref
):
    tokens, width = x_ref.shape[1:]
    heads = raw_ref.shape[2]
    head_dim = width // heads
    f32 = jnp.float32
    size, cum, _ = decays(limit_ref, raw_ref, bias_ref, rate_ref)
    last = cum[:, tokens - 1 : tokens]
    tail = spread((jnp.exp(last - cum) * size).T, head_dim)
    weighted = (tail * x_ref[0].astype(f32)).astype(jnp.bfloat16)
    b_t = b_ref[0, 0].astype(f32).T.astype(jnp.bfloat16)
    end_ref[0, 0] = jnp.dot(b_t, weighted, preferred_element_type=f32)
    grow = jnp.exp(cum.T)
    keep_ref[0, 0] = spread(jnp.broadcast_to(grow[tokens - 1 :], (8, heads)), head_dim)
    grow_ref[0, 0] = grow


def inside_kernel(
    limit_ref, x_ref, b_ref, c_ref, raw_ref, bias_ref, rate_ref, skip_ref, y_ref
):
    tokens, width = x_ref.shape[1:]
    heads = raw_ref.shape[2]
    head_dim = width // heads
    f32 = jnp.float32
    size, cum, causal = decays(limit_ref, raw_ref, bias_ref, rate_ref)
    cum_t = cum.T
    shifted = cum - jnp.where(size > 0, jnp.log(jnp.where(size > 0, size, 1.0)), far)
    scores = lax.dot_general(
        c_ref[0, 0], b_ref[0, 0], (((1,), (1,)), ((), ())), preferred_element_type=f32
    )
    lane = lax.broadcasted_iota(jnp.int32, (tokens, 2 * head_dim), 1)
    for pair in range(heads // 2):
        decayed = []
        for head in (2 * pair, 2 * pair + 1):
            gap = cum_t[:, head : head + 1] - shifted[head : head + 1, :]
            decayed.append((scores * jnp.exp(jnp.where(causal, gap, far))).astype(jnp.bfloat16))
        here = pl.ds(pair * 2 * head_dim, 2 * head_dim)
        x = x_ref[0, :, here]
        zero = jnp.zeros_like(x)
        apart = jnp.concatenate(
            [jnp.where(lane < head_dim, x, zero), jnp.where(lane >= head_dim, x, zero)], axis=0
        )
        y = jnp.dot(jnp.concatenate(decayed, axis=1), apart, preferred_element_type=f32)
        y_ref[0, :, here] = y + skip_ref[0, :, here] * x.astype(f32)


def local_specs(x, b, raw):
    tokens, width = x.shape[1], x.shape[2] // b.shape[1]
    state, heads = b.shape[3], raw.shape[2]

    def by_group(*block):
        return pl.BlockSpec((1, *block), lambda s, g, _: (g, 0, 0))

    def by_both(*block):
        return pl.BlockSpec((1, 1, *block), lambda s, g, _: (s, g, 0, 0))

    flat = pl.BlockSpec((1, tokens, width), lambda s, g, _: (s, 0, g))
    return (
        flat,
        by_both(tokens, state),
        by_both(heads, tokens),
        by_group(heads, 1),
        by_group(1, width),
    )


def end_part(limits, x, b, raw, bias, rate):
    sessions, tokens, inner = x.shape
    groups, state, heads = b.shape[1], b.shape[3], raw.shape[2]
    width = inner // groups
    flat, proj, per_token, per_head, _ = local_specs(x, b, raw)
    f32 = jnp.float32
    by_turn = lambda s, g, _: (g, s, 0, 0)
    return pl.pallas_call(
        end_kernel,
        grid_spec=pltpu.PrefetchScalarGridSpec(
            num_scalar_prefetch=1,
            grid=(sessions, groups),
            in_specs=[flat, proj, per_token, per_head, per_head],
            out_specs=[
                pl.BlockSpec((1, 1, state, width), by_turn),
                pl.BlockSpec((1, 1, 8, width), by_turn),
                pl.BlockSpec((1, 1, tokens, heads), lambda s, g, _: (s, g, 0, 0)),
            ],
        ),
        out_shape=[
            jax.ShapeDtypeStruct((groups, sessions, state, width), f32),
            jax.ShapeDtypeStruct((groups, sessions, 8, width), f32),
            jax.ShapeDtypeStruct((sessions, groups, tokens, heads), f32),
        ],
        compiler_params=pltpu.CompilerParams(vmem_limit_bytes=VMEM),
        cost_estimate=pl.CostEstimate(
            flops=2 * 10**9, bytes_accessed=8 * 2**20, transcendentals=2**18
        ),
        name="end_part",
    )(limits, x, b, raw, bias[:, :, None], rate[:, :, None])


def inside_part(limits, x, b, c, raw, bias, rate, skip):
    sessions, tokens, inner = x.shape
    groups = b.shape[1]
    flat, proj, per_token, per_head, per_channel = local_specs(x, b, raw)
    return pl.pallas_call(
        inside_kernel,
        grid_spec=pltpu.PrefetchScalarGridSpec(
            num_scalar_prefetch=1,
            grid=(sessions, groups),
            in_specs=[flat, proj, proj, per_token, per_head, per_head, per_channel],
            out_specs=flat,
        ),
        out_shape=jax.ShapeDtypeStruct((sessions, tokens, inner), jnp.float32),
        compiler_params=pltpu.CompilerParams(vmem_limit_bytes=VMEM),
        cost_estimate=pl.CostEstimate(
            flops=4 * 10**9, bytes_accessed=8 * 2**20, transcendentals=2**22
        ),
        name="inside_part",
    )(limits, x, b, c, raw, bias[:, :, None], rate[:, :, None], skip)


def leave_kernel(count, kind, *refs):
    at_ref, refs = refs[0], refs[1:]
    keep_ref, end_ref, state_ref, leaving_ref = refs[-4:]
    state = None
    if kind != "only":
        state = refs[0][0].astype(jnp.float32)
        refs = refs[1:]
    if count:
        first = jnp.concatenate([r[0, 0].astype(jnp.float32) for r in refs[:count]], axis=0)
        state = first if state is None else jnp.where(at_ref[1] == 0, first, state)
    state_ref[0] = state.astype(jnp.bfloat16)
    leaving_ref[0] = (keep_ref[0, 0, :1] * state + end_ref[0, 0]).astype(jnp.bfloat16)


def leave_part(at, coming, first, inside, keep, end):
    groups, sessions, state_size, width = end.shape
    by_turn = lambda s, at: (at[0], s, 0, 0)
    whole = pl.BlockSpec((1, state_size, width), lambda s, at: (s, 0, 0))
    operands, specs = [], []
    if coming is not None:
        operands.append(coming)
        specs.append(whole)
    if first is not None:
        operands += first
        specs += [
            pl.BlockSpec((1, 1, *f.shape[2:]), lambda s, at: (inside, s, 0, 0)) for f in first
        ]
    operands += [keep, end]
    specs += [
        pl.BlockSpec((1, 1, *keep.shape[2:]), by_turn),
        pl.BlockSpec((1, 1, state_size, width), by_turn),
    ]
    kind = None if first is None else ("only" if coming is None else "both")
    shape = jax.ShapeDtypeStruct((sessions, state_size, width), jnp.bfloat16)
    return pl.pallas_call(
        functools.partial(leave_kernel, 0 if first is None else len(first), kind),
        grid_spec=pltpu.PrefetchScalarGridSpec(
            num_scalar_prefetch=1, grid=(sessions,), in_specs=specs, out_specs=[whole, whole]
        ),
        out_shape=[shape, shape],
        compiler_params=pltpu.CompilerParams(vmem_limit_bytes=VMEM),
        cost_estimate=pl.CostEstimate(flops=10**6, bytes_accessed=3 * 2**20, transcendentals=0),
        name="leave_part",
    )(at, *operands)


def normed_kernel(at_ref, state_ref, c_ref, grow_ref, y_ref, gate_ref, gain_ref, _, out_ref):
    width = y_ref.shape[2]
    heads = grow_ref.shape[3]
    from_state = jnp.dot(c_ref[0, 0], state_ref[0], preferred_element_type=jnp.float32)
    ssd_out = y_ref[0] + from_state * spread(grow_ref[0, 0], width // heads)
    gate = gate_ref[0].astype(jnp.float32)
    gated = ssd_out * (gate / (1.0 + jnp.exp(-gate)))
    scale = lax.rsqrt(jnp.mean(gated * gated, axis=1, keepdims=True) + norm_eps)
    out_ref[0, 0] = (gated * scale * gain_ref[0]).astype(jnp.bfloat16)


def normed_part(index, at, state, c, grow, y, gate, gain, normed):
    sessions, tokens, inner = y.shape
    groups, state_size = c.shape[1], c.shape[3]
    width = inner // groups
    heads = grow.shape[3]
    by_both = lambda s, at: (s, at[0], 0, 0)
    flat = pl.BlockSpec((1, tokens, width), lambda s, at: (s, 0, at[0]))
    return pl.pallas_call(
        normed_kernel,
        grid_spec=pltpu.PrefetchScalarGridSpec(
            num_scalar_prefetch=1,
            grid=(sessions,),
            in_specs=[
                pl.BlockSpec((1, state_size, width), lambda s, at: (s, 0, 0)),
                pl.BlockSpec((1, 1, tokens, state_size), by_both),
                pl.BlockSpec((1, 1, tokens, heads), by_both),
                flat,
                flat,
                pl.BlockSpec((1, 1, width), lambda s, at: (at[0], 0, 0)),
                pl.BlockSpec(memory_space=pl.ANY),
            ],
            out_specs=pl.BlockSpec((1, 1, tokens, width), lambda s, at: (index, s, 0, 0)),
        ),
        out_shape=jax.ShapeDtypeStruct(normed.shape, normed.dtype),
        input_output_aliases={7: 0},
        compiler_params=pltpu.CompilerParams(vmem_limit_bytes=VMEM),
        cost_estimate=pl.CostEstimate(
            flops=10**8, bytes_accessed=4 * 2**20, transcendentals=2**19
        ),
        name="normed_part",
    )(at, state, c, grow, y, gate, gain, normed)


def pick_kernel(slot_ref, pool_ref, out_ref):
    heads, cols, head_dim = pool_ref.shape[1:]
    groups = out_ref.shape[0]
    per = heads // groups
    for g in range(groups):
        held = [pool_ref[0, g * per + h] for h in range(per)]
        out_ref[g, 0] = jnp.concatenate(held, axis=1).astype(jnp.bfloat16)


def pick_part(asked, pool, groups):
    _, heads, cols, head_dim = pool.shape
    count = asked.shape[0]
    width = heads // groups * head_dim
    return pl.pallas_call(
        pick_kernel,
        grid_spec=pltpu.PrefetchScalarGridSpec(
            num_scalar_prefetch=1,
            grid=(count,),
            in_specs=[pl.BlockSpec((1, heads, cols, head_dim), lambda i, slot: (slot[i], 0, 0, 0))],
            out_specs=pl.BlockSpec((groups, 1, cols, width), lambda i, slot: (0, i, 0, 0)),
        ),
        out_shape=jax.ShapeDtypeStruct((groups, count, cols, width), jnp.bfloat16),
        compiler_params=pltpu.CompilerParams(vmem_limit_bytes=VMEM),
        name="pick_part",
    )(asked, pool)


def final_kernel(value_ref, out_ref):
    heads, _, head_dim = out_ref.shape[1:]
    value = value_ref[0, 0].astype(jnp.float32)
    for h in range(heads):
        out_ref[0, h] = value[:, h * head_dim : (h + 1) * head_dim]


def final_part(value, heads, head_dim):
    groups, sessions, cols, width = value.shape
    per = heads // groups
    return pl.pallas_call(
        final_kernel,
        grid=(sessions, groups),
        in_specs=[pl.BlockSpec((1, 1, cols, width), lambda s, g: (g, s, 0, 0))],
        out_specs=pl.BlockSpec((1, per, cols, head_dim), lambda s, g: (s, g, 0, 0)),
        out_shape=jax.ShapeDtypeStruct((sessions, heads, cols, head_dim), jnp.float32),
        compiler_params=pltpu.CompilerParams(vmem_limit_bytes=VMEM),
        name="final_part",
    )(value)


def product_kernel(parts, base_ref, block_ref, *refs):
    lefts, weights, out_ref, held = refs[:parts], refs[parts:-2], refs[-2], refs[-1]

    @pl.when((pl.program_id(0) == 0) & (pl.program_id(1) == 0))
    def _():
        for k in range(parts):
            held[k] = lefts[k][0]

    total = jnp.zeros(out_ref.shape, jnp.float32)
    for k in range(parts):
        total += jnp.dot(held[k], weights[k][...], preferred_element_type=jnp.float32)
    out_ref[...] = total.astype(out_ref.dtype)


def product(base, blocks, lefts, gathered, row_at):
    parts = len(lefts)
    tokens, rows = lefts[0][0].shape[1:]
    count = blocks.shape[0]
    cols = gathered.shape[1]
    tile = min(cols, TILE)
    tiles = cols // tile

    def left_spec(place):
        return pl.BlockSpec((1, tokens, rows), lambda i, j, base, _: (place(base[0]), 0, 0))

    def weight_spec(k):
        return pl.BlockSpec((rows, tile), lambda i, j, _, blocks: (row_at(k, blocks[i]), j))

    return pl.pallas_call(
        functools.partial(product_kernel, parts),
        grid_spec=pltpu.PrefetchScalarGridSpec(
            num_scalar_prefetch=2,
            grid=(count, tiles),
            in_specs=[left_spec(place) for _, place in lefts]
            + [weight_spec(k) for k in range(parts)],
            out_specs=pl.BlockSpec((tokens, tile), lambda i, j, *_: (0, i * tiles + j)),
            scratch_shapes=[pltpu.VMEM((parts, tokens, rows), jnp.bfloat16)],
        ),
        out_shape=jax.ShapeDtypeStruct((tokens, count * cols), jnp.bfloat16),
        compiler_params=pltpu.CompilerParams(vmem_limit_bytes=VMEM),
        cost_estimate=pl.CostEstimate(
            flops=2 * tokens * parts * rows * cols * count,
            bytes_accessed=2 * (tokens * parts * rows + parts * rows * cols * count),
            transcendentals=0,
        ),
        name="product",
    )(
        base.reshape(1).astype(jnp.int32),
        blocks.astype(jnp.int32),
        *[left for left, _ in lefts],
        *[gathered] * parts,
    )


def shards(
    head_input,
    gate_input,
    state_in_proj,
    state_out_proj,
    step_raw,
    head_step_bias,
    decay_log,
    skip_gain,
    norm_gain,
    out_weight,
    pool_states,
    slot_map,
    span_lengths,
):
    turns = lax.axis_size("ctx")
    turn = lax.axis_index("ctx")
    lanes = lax.axis_size("groups")
    lane = lax.axis_index("groups")
    cores = lax.axis_size("sess")
    core = lax.axis_index("sess")
    head_count = lax.axis_size("head")
    head_index = lax.axis_index("head")
    sessions, tokens, inner = head_input.shape
    heads = step_raw.shape[2]
    head_dim = inner // heads
    slots = pool_states.shape[0]
    state_cols = pool_states.shape[3]
    groups = heads // GROUP_HEADS
    width = inner // groups
    bf16 = jnp.bfloat16

    carriers = lanes * cores
    rows = inner // carriers
    mine = lax.dynamic_slice_in_dim(out_weight, (lane * cores + core) * rows, rows, 0)
    gathered = lax.all_gather(mine, ("groups", "ctx", "sess"), axis=0, tiled=True)

    def row_at(k, q):
        return (k // cores * turns + q) * cores + k % cores

    def slots_of(which):
        return lax.dynamic_slice_in_dim(slot_map, which * sessions, sessions)

    own_slots = slots_of(core)
    asked = jnp.concatenate([slots_of((core - by) % cores) for by in range(cores)])
    picked = pick_part(asked % slots, pool_states.transpose(0, 1, 3, 2), groups)
    start = picked[:, :sessions]
    for by in range(1, cores):
        found = picked[:, by * sessions : (by + 1) * sessions]
        found = lax.ppermute(found, "sess", [(i, (i - by) % cores) for i in range(cores)])
        here = (own_slots // slots == (core + by) % cores)[None, :, None, None]
        start = jnp.where(here, found, start)
    entering = []
    for g in range(groups):
        part = start[g : g + 1]
        if g:
            part, entering[-1] = lax.optimization_barrier((part, entering[-1]))
        entering.append([part] + [lax.ppermute(part, "ctx", [(k, 0)]) for k in range(1, turns)])

    first_session = core * sessions
    own_lengths = lax.dynamic_slice_in_dim(span_lengths, first_session, sessions)
    limits = jnp.clip(own_lengths * SPAN - turn * tokens, 0, tokens)
    first_group = head_index * groups

    def grouped(proj):
        return lax.dynamic_slice_in_dim(proj, first_group, groups, 2).swapaxes(1, 2)

    b = grouped(state_in_proj)
    c = grouped(state_out_proj)
    raw = step_raw.swapaxes(1, 2).reshape(sessions, groups, GROUP_HEADS, tokens)
    skip = jnp.repeat(skip_gain, head_dim).reshape(groups, 1, width)
    gain = norm_gain.reshape(groups, 1, width)
    bias = head_step_bias.reshape(groups, GROUP_HEADS)
    rate = decay_log.reshape(groups, GROUP_HEADS)
    end, keep, grow = end_part(limits, head_input, b, raw, bias, rate)

    waves = groups + turns - 2
    normed = jnp.zeros((waves + 1, sessions, tokens, width), bf16)
    leavings = []
    coming = None
    for index in range(waves + 1):
        at = jnp.stack([jnp.clip(index - turn, 0, groups - 1), turn]).astype(jnp.int32)
        given = entering[index] if index < groups else None
        state, leaving = leave_part(at, coming, given, 0, keep, end)
        leavings.append(leaving)
        if index < waves:
            pairs = [(i, i + 1) for i in range(turns - 1) if 0 <= index - i < groups]
            coming = lax.ppermute(leaving, "ctx", pairs)
        if index == 0:
            x, state = lax.optimization_barrier((head_input, state))
            y = inside_part(limits, x, b, c, raw, bias, rate, skip)
        normed = normed_part(index, at, state, c, grow, y, gate_input, gain, normed)
        if index < waves:
            coming, normed = lax.optimization_barrier((coming, normed))

    final = jnp.stack(leavings[turns - 1 :])

    def moved(final, step):
        by = turns // 2 ** (step + 1)
        half = final.shape[2] // 2
        pairs = [(z, z - by) for z in range(turns) if (turns - 1 - z) % (2 * by) == 0]
        return lax.ppermute(final[:, :, :half], "ctx", pairs)

    def placed(final, got, step):
        by = turns // 2 ** (step + 1)
        half = final.shape[2] // 2
        return jnp.where((turns - 1 - turn) % (2 * by) == by, got, final[:, :, half:])

    steps = (turns - 1).bit_length()

    def at_place(k):
        return lambda base: base + k

    def at_fixed(k):
        return lambda base: k

    if groups == carriers:
        held = normed.reshape(waves + 1, sessions * tokens, width)
        left = [(held, at_place(k)) for k in range(carriers)]
    else:
        held = lax.dynamic_slice_in_dim(normed, turn, groups, 0)
        held = held.reshape(groups, sessions * tokens, width)
        held = held.transpose(1, 0, 2).reshape(sessions * tokens, carriers, rows)
        held = held.transpose(1, 0, 2)
        left = [(held, at_fixed(k)) for k in range(carriers)]
    live = (jnp.arange(tokens, dtype=jnp.int32)[None, :] < limits[:, None]).astype(jnp.float32)
    if head_count == 2:
        share = turns // 2
        theirs = []
        got = moved(final, 0)
        for m in range(share):
            block = product(turn, ((1 - head_index) * share + m).reshape(1), left, gathered, row_at)
            if m < steps:
                got, block = lax.optimization_barrier((got, block))
                final = placed(final, got, m)
                if m + 1 < steps:
                    got = moved(final, m + 1)
            theirs.append(lax.ppermute(block, "head", [(0, 1), (1, 0)]))
        ours = product(turn, head_index * share + jnp.arange(share), left, gathered, row_at)
        for step in range(share, steps):
            final = placed(final, moved(final, step), step)
        final, ours = lax.optimization_barrier((final, ours))
        final = final_part(final, heads, head_dim)
        theirs, ours, final = lax.optimization_barrier((theirs, ours, final))
        summed = ours.astype(jnp.float32) + jnp.concatenate(theirs, axis=1).astype(jnp.float32)
        summed = summed.reshape(sessions, tokens, -1)
    else:
        for step in range(steps):
            final = placed(final, moved(final, step), step)
        final = final_part(final, heads, head_dim)
        partial = product(turn, jnp.arange(turns), left, gathered, row_at)
        partial = partial.reshape(sessions, tokens, -1)
        summed = lax.psum_scatter(partial, "head", scatter_dimension=2, tiled=True).astype(
            jnp.float32
        )
    mixed = (summed * live[:, :, None]).astype(bf16)
    return (mixed, final.transpose(0, 1, 3, 2))


def solution(mesh):
    placed = (
        P(("groups", "sess"), "ctx", "head"),
        P(("groups", "sess"), "ctx", "head"),
        P(("groups", "sess"), "ctx", None, None),
        P(("groups", "sess"), "ctx", None, None),
        P(("groups", "sess"), "ctx", "head"),
        P("head"),
        P("head"),
        P("head"),
        P("head"),
        P("head", "ctx"),
        P(("groups", "sess"), "head", None, "ctx"),
        P("groups"),
        P("groups"),
    )
    return jax.shard_map(
        shards,
        mesh=mesh,
        in_specs=placed,
        out_specs=(
            P(("groups", "sess"), "ctx", "head"),
            P(("groups", "sess"), "head", None, "ctx"),
        ),
        check_vma=False,
    )
```

```python
import functools

import jax
import jax.numpy as jnp
from jax import lax
from jax.experimental import pallas as pl
from jax.experimental.pallas import tpu as pltpu
from jax.sharding import PartitionSpec as P

HEADS = 128
GROUPS = 8
SPAN = 128
GROUP_HEADS = HEADS // GROUPS
TILE = 512
VMEM = 20 * 1024 * 1024

norm_eps = 1e-05
far = -1e30


def spread(values, head_dim):
    heads = values.shape[1]
    high = values.astype(jnp.bfloat16)
    low = (values - high.astype(jnp.float32)).astype(jnp.bfloat16)
    both = jnp.concatenate([high, low], axis=1)
    row = lax.broadcasted_iota(jnp.int32, (2 * heads, heads * head_dim), 0)
    col = lax.broadcasted_iota(jnp.int32, (2 * heads, heads * head_dim), 1)
    ones = (col // head_dim == row % heads).astype(jnp.bfloat16)
    return jnp.dot(both, ones, preferred_element_type=jnp.float32)


def decays(limit_ref, raw_ref, bias_ref, rate_ref):
    heads, tokens = raw_ref.shape[2:]
    f32 = jnp.float32
    token = lax.broadcasted_iota(jnp.int32, (heads, tokens), 1)
    size = jax.nn.softplus(raw_ref[0, 0] + bias_ref[0])
    size = size * (token < limit_ref[pl.program_id(0)]).astype(f32)
    log_keep = -jnp.exp(rate_ref[0]) * size
    row = lax.broadcasted_iota(jnp.int32, (tokens, tokens), 0)
    col = lax.broadcasted_iota(jnp.int32, (tokens, tokens), 1)
    cum = jnp.dot(log_keep, (row <= col).astype(f32), precision=lax.Precision.HIGHEST)
    return size, cum, row >= col


def end_kernel(
    limit_ref, x_ref, b_ref, raw_ref, bias_ref, rate_ref, end_ref, keep_ref, grow_ref
):
    tokens, width = x_ref.shape[1:]
    heads = raw_ref.shape[2]
    head_dim = width // heads
    f32 = jnp.float32
    size, cum, _ = decays(limit_ref, raw_ref, bias_ref, rate_ref)
    last = cum[:, tokens - 1 : tokens]
    tail = spread((jnp.exp(last - cum) * size).T, head_dim)
    weighted = (tail * x_ref[0].astype(f32)).astype(jnp.bfloat16)
    b_t = b_ref[0, 0].astype(f32).T.astype(jnp.bfloat16)
    end_ref[0, 0] = jnp.dot(b_t, weighted, preferred_element_type=f32)
    grow = jnp.exp(cum.T)
    keep_ref[0, 0] = spread(jnp.broadcast_to(grow[tokens - 1 :], (8, heads)), head_dim)
    grow_ref[0, 0] = grow


def inside_kernel(
    limit_ref, x_ref, b_ref, c_ref, raw_ref, bias_ref, rate_ref, skip_ref, y_ref
):
    tokens, width = x_ref.shape[1:]
    heads = raw_ref.shape[2]
    head_dim = width // heads
    f32 = jnp.float32
    size, cum, causal = decays(limit_ref, raw_ref, bias_ref, rate_ref)
    cum_t = cum.T
    shifted = cum - jnp.where(size > 0, jnp.log(jnp.where(size > 0, size, 1.0)), far)
    scores = lax.dot_general(
        c_ref[0, 0], b_ref[0, 0], (((1,), (1,)), ((), ())), preferred_element_type=f32
    )
    lane = lax.broadcasted_iota(jnp.int32, (tokens, 2 * head_dim), 1)
    for pair in range(heads // 2):
        decayed = []
        for head in (2 * pair, 2 * pair + 1):
            gap = cum_t[:, head : head + 1] - shifted[head : head + 1, :]
            decayed.append((scores * jnp.exp(jnp.where(causal, gap, far))).astype(jnp.bfloat16))
        here = pl.ds(pair * 2 * head_dim, 2 * head_dim)
        x = x_ref[0, :, here]
        zero = jnp.zeros_like(x)
        apart = jnp.concatenate(
            [jnp.where(lane < head_dim, x, zero), jnp.where(lane >= head_dim, x, zero)], axis=0
        )
        y = jnp.dot(jnp.concatenate(decayed, axis=1), apart, preferred_element_type=f32)
        y_ref[0, :, here] = y + skip_ref[0, :, here] * x.astype(f32)


def local_specs(x, b, raw):
    tokens, width = x.shape[1], x.shape[2] // b.shape[1]
    state, heads = b.shape[3], raw.shape[2]

    def by_group(*block):
        return pl.BlockSpec((1, *block), lambda s, g, _: (g, 0, 0))

    def by_both(*block):
        return pl.BlockSpec((1, 1, *block), lambda s, g, _: (s, g, 0, 0))

    flat = pl.BlockSpec((1, tokens, width), lambda s, g, _: (s, 0, g))
    return (
        flat,
        by_both(tokens, state),
        by_both(heads, tokens),
        by_group(heads, 1),
        by_group(1, width),
    )


def end_part(limits, x, b, raw, bias, rate):
    sessions, tokens, inner = x.shape
    groups, state, heads = b.shape[1], b.shape[3], raw.shape[2]
    width = inner // groups
    flat, proj, per_token, per_head, _ = local_specs(x, b, raw)
    f32 = jnp.float32
    by_turn = lambda s, g, _: (g, s, 0, 0)
    return pl.pallas_call(
        end_kernel,
        grid_spec=pltpu.PrefetchScalarGridSpec(
            num_scalar_prefetch=1,
            grid=(sessions, groups),
            in_specs=[flat, proj, per_token, per_head, per_head],
            out_specs=[
                pl.BlockSpec((1, 1, state, width), by_turn),
                pl.BlockSpec((1, 1, 8, width), by_turn),
                pl.BlockSpec((1, 1, tokens, heads), lambda s, g, _: (s, g, 0, 0)),
            ],
        ),
        out_shape=[
            jax.ShapeDtypeStruct((groups, sessions, state, width), f32),
            jax.ShapeDtypeStruct((groups, sessions, 8, width), f32),
            jax.ShapeDtypeStruct((sessions, groups, tokens, heads), f32),
        ],
        compiler_params=pltpu.CompilerParams(vmem_limit_bytes=VMEM),
        cost_estimate=pl.CostEstimate(
            flops=2 * 10**9, bytes_accessed=8 * 2**20, transcendentals=2**18
        ),
        name="end_part",
    )(limits, x, b, raw, bias[:, :, None], rate[:, :, None])


def inside_part(limits, x, b, c, raw, bias, rate, skip):
    sessions, tokens, inner = x.shape
    groups = b.shape[1]
    flat, proj, per_token, per_head, per_channel = local_specs(x, b, raw)
    return pl.pallas_call(
        inside_kernel,
        grid_spec=pltpu.PrefetchScalarGridSpec(
            num_scalar_prefetch=1,
            grid=(sessions, groups),
            in_specs=[flat, proj, proj, per_token, per_head, per_head, per_channel],
            out_specs=flat,
        ),
        out_shape=jax.ShapeDtypeStruct((sessions, tokens, inner), jnp.float32),
        compiler_params=pltpu.CompilerParams(vmem_limit_bytes=VMEM),
        cost_estimate=pl.CostEstimate(
            flops=4 * 10**9, bytes_accessed=8 * 2**20, transcendentals=2**22
        ),
        name="inside_part",
    )(limits, x, b, c, raw, bias[:, :, None], rate[:, :, None], skip)


def leave_kernel(count, kind, *refs):
    at_ref, refs = refs[0], refs[1:]
    keep_ref, end_ref, state_ref, leaving_ref = refs[-4:]
    state = None
    if kind != "only":
        state = refs[0][0].astype(jnp.float32)
        refs = refs[1:]
    if count:
        first = jnp.concatenate([r[0, 0].astype(jnp.float32) for r in refs[:count]], axis=0)
        state = first if state is None else jnp.where(at_ref[1] == 0, first, state)
    state_ref[0] = state.astype(jnp.bfloat16)
    leaving_ref[0] = (keep_ref[0, 0, :1] * state + end_ref[0, 0]).astype(jnp.bfloat16)


def leave_part(at, coming, first, inside, keep, end):
    groups, sessions, state_size, width = end.shape
    by_turn = lambda s, at: (at[0], s, 0, 0)
    whole = pl.BlockSpec((1, state_size, width), lambda s, at: (s, 0, 0))
    operands, specs = [], []
    if coming is not None:
        operands.append(coming)
        specs.append(whole)
    if first is not None:
        operands += first
        specs += [
            pl.BlockSpec((1, 1, *f.shape[2:]), lambda s, at: (inside, s, 0, 0)) for f in first
        ]
    operands += [keep, end]
    specs += [
        pl.BlockSpec((1, 1, *keep.shape[2:]), by_turn),
        pl.BlockSpec((1, 1, state_size, width), by_turn),
    ]
    kind = None if first is None else ("only" if coming is None else "both")
    shape = jax.ShapeDtypeStruct((sessions, state_size, width), jnp.bfloat16)
    return pl.pallas_call(
        functools.partial(leave_kernel, 0 if first is None else len(first), kind),
        grid_spec=pltpu.PrefetchScalarGridSpec(
            num_scalar_prefetch=1, grid=(sessions,), in_specs=specs, out_specs=[whole, whole]
        ),
        out_shape=[shape, shape],
        compiler_params=pltpu.CompilerParams(vmem_limit_bytes=VMEM),
        cost_estimate=pl.CostEstimate(flops=10**6, bytes_accessed=3 * 2**20, transcendentals=0),
        name="leave_part",
    )(at, *operands)


def normed_kernel(at_ref, state_ref, c_ref, grow_ref, y_ref, gate_ref, gain_ref, _, out_ref):
    width = y_ref.shape[2]
    heads = grow_ref.shape[3]
    from_state = jnp.dot(c_ref[0, 0], state_ref[0], preferred_element_type=jnp.float32)
    ssd_out = y_ref[0] + from_state * spread(grow_ref[0, 0], width // heads)
    gate = gate_ref[0].astype(jnp.float32)
    gated = ssd_out * (gate / (1.0 + jnp.exp(-gate)))
    scale = lax.rsqrt(jnp.mean(gated * gated, axis=1, keepdims=True) + norm_eps)
    out_ref[0, 0] = (gated * scale * gain_ref[0]).astype(jnp.bfloat16)


def normed_part(index, at, state, c, grow, y, gate, gain, normed):
    sessions, tokens, inner = y.shape
    groups, state_size = c.shape[1], c.shape[3]
    width = inner // groups
    heads = grow.shape[3]
    by_both = lambda s, at: (s, at[0], 0, 0)
    flat = pl.BlockSpec((1, tokens, width), lambda s, at: (s, 0, at[0]))
    return pl.pallas_call(
        normed_kernel,
        grid_spec=pltpu.PrefetchScalarGridSpec(
            num_scalar_prefetch=1,
            grid=(sessions,),
            in_specs=[
                pl.BlockSpec((1, state_size, width), lambda s, at: (s, 0, 0)),
                pl.BlockSpec((1, 1, tokens, state_size), by_both),
                pl.BlockSpec((1, 1, tokens, heads), by_both),
                flat,
                flat,
                pl.BlockSpec((1, 1, width), lambda s, at: (at[0], 0, 0)),
                pl.BlockSpec(memory_space=pl.ANY),
            ],
            out_specs=pl.BlockSpec((1, 1, tokens, width), lambda s, at: (index, s, 0, 0)),
        ),
        out_shape=jax.ShapeDtypeStruct(normed.shape, normed.dtype),
        input_output_aliases={7: 0},
        compiler_params=pltpu.CompilerParams(vmem_limit_bytes=VMEM),
        cost_estimate=pl.CostEstimate(
            flops=10**8, bytes_accessed=4 * 2**20, transcendentals=2**19
        ),
        name="normed_part",
    )(at, state, c, grow, y, gate, gain, normed)


def pick_kernel(slot_ref, pool_ref, out_ref):
    heads, cols, head_dim = pool_ref.shape[1:]
    groups = out_ref.shape[0]
    per = heads // groups
    for g in range(groups):
        held = [pool_ref[0, g * per + h] for h in range(per)]
        out_ref[g, 0] = jnp.concatenate(held, axis=1).astype(jnp.bfloat16)


def pick_part(asked, pool, groups):
    _, heads, cols, head_dim = pool.shape
    count = asked.shape[0]
    width = heads // groups * head_dim
    return pl.pallas_call(
        pick_kernel,
        grid_spec=pltpu.PrefetchScalarGridSpec(
            num_scalar_prefetch=1,
            grid=(count,),
            in_specs=[pl.BlockSpec((1, heads, cols, head_dim), lambda i, slot: (slot[i], 0, 0, 0))],
            out_specs=pl.BlockSpec((groups, 1, cols, width), lambda i, slot: (0, i, 0, 0)),
        ),
        out_shape=jax.ShapeDtypeStruct((groups, count, cols, width), jnp.bfloat16),
        compiler_params=pltpu.CompilerParams(vmem_limit_bytes=VMEM),
        name="pick_part",
    )(asked, pool)


def final_kernel(value_ref, out_ref):
    heads, _, head_dim = out_ref.shape[1:]
    value = value_ref[0, 0].astype(jnp.float32)
    for h in range(heads):
        out_ref[0, h] = value[:, h * head_dim : (h + 1) * head_dim]


def final_part(value, heads, head_dim):
    groups, sessions, cols, width = value.shape
    per = heads // groups
    return pl.pallas_call(
        final_kernel,
        grid=(sessions, groups),
        in_specs=[pl.BlockSpec((1, 1, cols, width), lambda s, g: (g, s, 0, 0))],
        out_specs=pl.BlockSpec((1, per, cols, head_dim), lambda s, g: (s, g, 0, 0)),
        out_shape=jax.ShapeDtypeStruct((sessions, heads, cols, head_dim), jnp.float32),
        compiler_params=pltpu.CompilerParams(vmem_limit_bytes=VMEM),
        name="final_part",
    )(value)


def product_kernel(parts, base_ref, block_ref, *refs):
    lefts, weights, out_ref, held = refs[:parts], refs[parts:-2], refs[-2], refs[-1]

    @pl.when((pl.program_id(0) == 0) & (pl.program_id(1) == 0))
    def _():
        for k in range(parts):
            held[k] = lefts[k][0]

    total = jnp.zeros(out_ref.shape, jnp.float32)
    for k in range(parts):
        total += jnp.dot(held[k], weights[k][...], preferred_element_type=jnp.float32)
    out_ref[...] = total.astype(out_ref.dtype)


def product(base, blocks, lefts, gathered, row_at):
    parts = len(lefts)
    tokens, rows = lefts[0][0].shape[1:]
    count = blocks.shape[0]
    cols = gathered.shape[1]
    tile = min(cols, TILE)
    tiles = cols // tile

    def left_spec(place):
        return pl.BlockSpec((1, tokens, rows), lambda i, j, base, _: (place(base[0]), 0, 0))

    def weight_spec(k):
        return pl.BlockSpec((rows, tile), lambda i, j, _, blocks: (row_at(k, blocks[i]), j))

    return pl.pallas_call(
        functools.partial(product_kernel, parts),
        grid_spec=pltpu.PrefetchScalarGridSpec(
            num_scalar_prefetch=2,
            grid=(count, tiles),
            in_specs=[left_spec(place) for _, place in lefts]
            + [weight_spec(k) for k in range(parts)],
            out_specs=pl.BlockSpec((tokens, tile), lambda i, j, *_: (0, i * tiles + j)),
            scratch_shapes=[pltpu.VMEM((parts, tokens, rows), jnp.bfloat16)],
        ),
        out_shape=jax.ShapeDtypeStruct((tokens, count * cols), jnp.bfloat16),
        compiler_params=pltpu.CompilerParams(vmem_limit_bytes=VMEM),
        cost_estimate=pl.CostEstimate(
            flops=2 * tokens * parts * rows * cols * count,
            bytes_accessed=2 * (tokens * parts * rows + parts * rows * cols * count),
            transcendentals=0,
        ),
        name="product",
    )(
        base.reshape(1).astype(jnp.int32),
        blocks.astype(jnp.int32),
        *[left for left, _ in lefts],
        *[gathered] * parts,
    )


def shards(
    head_input,
    gate_input,
    state_in_proj,
    state_out_proj,
    step_raw,
    head_step_bias,
    decay_log,
    skip_gain,
    norm_gain,
    out_weight,
    pool_states,
    slot_map,
    span_lengths,
):
    turns = lax.axis_size("ctx")
    turn = lax.axis_index("ctx")
    lanes = lax.axis_size("groups")
    lane = lax.axis_index("groups")
    cores = lax.axis_size("sess")
    core = lax.axis_index("sess")
    head_count = lax.axis_size("head")
    head_index = lax.axis_index("head")
    sessions, tokens, inner = head_input.shape
    heads = step_raw.shape[2]
    head_dim = inner // heads
    slots = pool_states.shape[0]
    state_cols = pool_states.shape[3]
    groups = heads // GROUP_HEADS
    width = inner // groups
    bf16 = jnp.bfloat16

    carriers = lanes * cores
    rows = inner // carriers
    mine = lax.dynamic_slice_in_dim(out_weight, (lane * cores + core) * rows, rows, 0)
    gathered = lax.all_gather(mine, ("groups", "ctx", "sess"), axis=0, tiled=True)

    def row_at(k, q):
        return (k // cores * turns + q) * cores + k % cores

    def slots_of(which):
        return lax.dynamic_slice_in_dim(slot_map, which * sessions, sessions)

    own_slots = slots_of(core)
    asked = jnp.concatenate([slots_of((core - by) % cores) for by in range(cores)])
    picked = pick_part(asked % slots, pool_states.transpose(0, 1, 3, 2), groups)
    start = picked[:, :sessions]
    for by in range(1, cores):
        found = picked[:, by * sessions : (by + 1) * sessions]
        found = lax.ppermute(found, "sess", [(i, (i - by) % cores) for i in range(cores)])
        here = (own_slots // slots == (core + by) % cores)[None, :, None, None]
        start = jnp.where(here, found, start)
    entering = []
    for g in range(groups):
        part = start[g : g + 1]
        if g:
            part, entering[-1] = lax.optimization_barrier((part, entering[-1]))
        entering.append([part] + [lax.ppermute(part, "ctx", [(k, 0)]) for k in range(1, turns)])

    first_session = core * sessions
    own_lengths = lax.dynamic_slice_in_dim(span_lengths, first_session, sessions)
    limits = jnp.clip(own_lengths * SPAN - turn * tokens, 0, tokens)
    first_group = head_index * groups

    def grouped(proj):
        return lax.dynamic_slice_in_dim(proj, first_group, groups, 2).swapaxes(1, 2)

    b = grouped(state_in_proj)
    c = grouped(state_out_proj)
    raw = step_raw.swapaxes(1, 2).reshape(sessions, groups, GROUP_HEADS, tokens)
    skip = jnp.repeat(skip_gain, head_dim).reshape(groups, 1, width)
    gain = norm_gain.reshape(groups, 1, width)
    bias = head_step_bias.reshape(groups, GROUP_HEADS)
    rate = decay_log.reshape(groups, GROUP_HEADS)
    end, keep, grow = end_part(limits, head_input, b, raw, bias, rate)

    waves = groups + turns - 2
    normed = jnp.zeros((waves + 1, sessions, tokens, width), bf16)
    leavings = []
    coming = None
    for index in range(waves + 1):
        at = jnp.stack([jnp.clip(index - turn, 0, groups - 1), turn]).astype(jnp.int32)
        given = entering[index] if index < groups else None
        state, leaving = leave_part(at, coming, given, 0, keep, end)
        leavings.append(leaving)
        if index < waves:
            pairs = [(i, i + 1) for i in range(turns - 1) if 0 <= index - i < groups]
            coming = lax.ppermute(leaving, "ctx", pairs)
        if index == 0:
            x, state = lax.optimization_barrier((head_input, state))
            y = inside_part(limits, x, b, c, raw, bias, rate, skip)
        normed = normed_part(index, at, state, c, grow, y, gate_input, gain, normed)
        if index < waves:
            coming, normed = lax.optimization_barrier((coming, normed))

    final = jnp.stack(leavings[turns - 1 :])

    def moved(final, step):
        by = turns // 2 ** (step + 1)
        half = final.shape[2] // 2
        pairs = [(z, z - by) for z in range(turns) if (turns - 1 - z) % (2 * by) == 0]
        return lax.ppermute(final[:, :, :half], "ctx", pairs)

    def placed(final, got, step):
        by = turns // 2 ** (step + 1)
        half = final.shape[2] // 2
        return jnp.where((turns - 1 - turn) % (2 * by) == by, got, final[:, :, half:])

    steps = (turns - 1).bit_length()

    def at_place(k):
        return lambda base: base + k

    def at_fixed(k):
        return lambda base: k

    if groups == carriers:
        held = normed.reshape(waves + 1, sessions * tokens, width)
        left = [(held, at_place(k)) for k in range(carriers)]
    else:
        held = lax.dynamic_slice_in_dim(normed, turn, groups, 0)
        held = held.reshape(groups, sessions * tokens, width)
        held = held.transpose(1, 0, 2).reshape(sessions * tokens, carriers, rows)
        held = held.transpose(1, 0, 2)
        left = [(held, at_fixed(k)) for k in range(carriers)]
    live = (jnp.arange(tokens, dtype=jnp.int32)[None, :] < limits[:, None]).astype(jnp.float32)
    if head_count == 2:
        share = turns // 2
        theirs = []
        got = moved(final, 0)
        for m in range(share):
            block = product(turn, ((1 - head_index) * share + m).reshape(1), left, gathered, row_at)
            theirs.append(lax.ppermute(block, "head", [(0, 1), (1, 0)]))
            if m == 0:
                got, _ = lax.optimization_barrier((got, block))
                final = placed(final, got, 0)
        ours = product(turn, head_index * share + jnp.arange(share), left, gathered, row_at)
        for step in range(1, steps):
            got = moved(final, step)
            got, ours = lax.optimization_barrier((got, ours))
            final = placed(final, got, step)
        final = final_part(final, heads, head_dim)
        theirs, ours, final = lax.optimization_barrier((theirs, ours, final))
        summed = ours.astype(jnp.float32) + jnp.concatenate(theirs, axis=1).astype(jnp.float32)
        summed = summed.reshape(sessions, tokens, -1)
    else:
        for step in range(steps):
            final = placed(final, moved(final, step), step)
        final = final_part(final, heads, head_dim)
        partial = product(turn, jnp.arange(turns), left, gathered, row_at)
        partial = partial.reshape(sessions, tokens, -1)
        summed = lax.psum_scatter(partial, "head", scatter_dimension=2, tiled=True).astype(
            jnp.float32
        )
    mixed = (summed * live[:, :, None]).astype(bf16)
    return (mixed, final.transpose(0, 1, 3, 2))


def solution(mesh):
    placed = (
        P(("groups", "sess"), "ctx", "head"),
        P(("groups", "sess"), "ctx", "head"),
        P(("groups", "sess"), "ctx", None, None),
        P(("groups", "sess"), "ctx", None, None),
        P(("groups", "sess"), "ctx", "head"),
        P("head"),
        P("head"),
        P("head"),
        P("head"),
        P("head", "ctx"),
        P(("groups", "sess"), "head", None, "ctx"),
        P("groups"),
        P("groups"),
    )
    return jax.shard_map(
        shards,
        mesh=mesh,
        in_specs=placed,
        out_specs=(
            P(("groups", "sess"), "ctx", "head"),
            P(("groups", "sess"), "head", None, "ctx"),
        ),
        check_vma=False,
    )
```

```python
import functools

import jax
import jax.numpy as jnp
from jax import lax
from jax.experimental import pallas as pl
from jax.experimental.pallas import tpu as pltpu
from jax.sharding import PartitionSpec as P

HEADS = 128
GROUPS = 8
SPAN = 128
GROUP_HEADS = HEADS // GROUPS
TILE = 512
VMEM = 20 * 1024 * 1024

norm_eps = 1e-05
far = -1e30


def spread(values, head_dim):
    heads = values.shape[1]
    high = values.astype(jnp.bfloat16)
    low = (values - high.astype(jnp.float32)).astype(jnp.bfloat16)
    both = jnp.concatenate([high, low], axis=1)
    row = lax.broadcasted_iota(jnp.int32, (2 * heads, heads * head_dim), 0)
    col = lax.broadcasted_iota(jnp.int32, (2 * heads, heads * head_dim), 1)
    ones = (col // head_dim == row % heads).astype(jnp.bfloat16)
    return jnp.dot(both, ones, preferred_element_type=jnp.float32)


def decays(limit_ref, raw_ref, bias_ref, rate_ref):
    heads, tokens = raw_ref.shape[2:]
    f32 = jnp.float32
    token = lax.broadcasted_iota(jnp.int32, (heads, tokens), 1)
    size = jax.nn.softplus(raw_ref[0, 0] + bias_ref[0])
    size = size * (token < limit_ref[pl.program_id(0)]).astype(f32)
    log_keep = -jnp.exp(rate_ref[0]) * size
    row = lax.broadcasted_iota(jnp.int32, (tokens, tokens), 0)
    col = lax.broadcasted_iota(jnp.int32, (tokens, tokens), 1)
    cum = jnp.dot(log_keep, (row <= col).astype(f32), precision=lax.Precision.HIGHEST)
    return size, cum, row >= col


def end_kernel(
    limit_ref, x_ref, b_ref, raw_ref, bias_ref, rate_ref, end_ref, keep_ref, grow_ref
):
    tokens, width = x_ref.shape[1:]
    heads = raw_ref.shape[2]
    head_dim = width // heads
    f32 = jnp.float32
    size, cum, _ = decays(limit_ref, raw_ref, bias_ref, rate_ref)
    last = cum[:, tokens - 1 : tokens]
    tail = spread((jnp.exp(last - cum) * size).T, head_dim)
    weighted = (tail * x_ref[0].astype(f32)).astype(jnp.bfloat16)
    b_t = b_ref[0, 0].astype(f32).T.astype(jnp.bfloat16)
    end_ref[0, 0] = jnp.dot(b_t, weighted, preferred_element_type=f32)
    grow = jnp.exp(cum.T)
    keep_ref[0, 0] = spread(jnp.broadcast_to(grow[tokens - 1 :], (8, heads)), head_dim)
    grow_ref[0, 0] = grow


def inside_kernel(
    limit_ref, x_ref, b_ref, c_ref, raw_ref, bias_ref, rate_ref, skip_ref, y_ref
):
    tokens, width = x_ref.shape[1:]
    heads = raw_ref.shape[2]
    head_dim = width // heads
    f32 = jnp.float32
    size, cum, causal = decays(limit_ref, raw_ref, bias_ref, rate_ref)
    cum_t = cum.T
    shifted = cum - jnp.where(size > 0, jnp.log(jnp.where(size > 0, size, 1.0)), far)
    scores = lax.dot_general(
        c_ref[0, 0], b_ref[0, 0], (((1,), (1,)), ((), ())), preferred_element_type=f32
    )
    lane = lax.broadcasted_iota(jnp.int32, (tokens, 2 * head_dim), 1)
    for pair in range(heads // 2):
        decayed = []
        for head in (2 * pair, 2 * pair + 1):
            gap = cum_t[:, head : head + 1] - shifted[head : head + 1, :]
            decayed.append((scores * jnp.exp(jnp.where(causal, gap, far))).astype(jnp.bfloat16))
        here = pl.ds(pair * 2 * head_dim, 2 * head_dim)
        x = x_ref[0, :, here]
        zero = jnp.zeros_like(x)
        apart = jnp.concatenate(
            [jnp.where(lane < head_dim, x, zero), jnp.where(lane >= head_dim, x, zero)], axis=0
        )
        y = jnp.dot(jnp.concatenate(decayed, axis=1), apart, preferred_element_type=f32)
        y_ref[0, :, here] = y + skip_ref[0, :, here] * x.astype(f32)


def local_specs(x, b, raw):
    tokens, width = x.shape[1], x.shape[2] // b.shape[1]
    state, heads = b.shape[3], raw.shape[2]

    def by_group(*block):
        return pl.BlockSpec((1, *block), lambda s, g, _: (g, 0, 0))

    def by_both(*block):
        return pl.BlockSpec((1, 1, *block), lambda s, g, _: (s, g, 0, 0))

    flat = pl.BlockSpec((1, tokens, width), lambda s, g, _: (s, 0, g))
    return (
        flat,
        by_both(tokens, state),
        by_both(heads, tokens),
        by_group(heads, 1),
        by_group(1, width),
    )


def end_part(limits, x, b, raw, bias, rate):
    sessions, tokens, inner = x.shape
    groups, state, heads = b.shape[1], b.shape[3], raw.shape[2]
    width = inner // groups
    flat, proj, per_token, per_head, _ = local_specs(x, b, raw)
    f32 = jnp.float32
    by_turn = lambda s, g, _: (g, s, 0, 0)
    return pl.pallas_call(
        end_kernel,
        grid_spec=pltpu.PrefetchScalarGridSpec(
            num_scalar_prefetch=1,
            grid=(sessions, groups),
            in_specs=[flat, proj, per_token, per_head, per_head],
            out_specs=[
                pl.BlockSpec((1, 1, state, width), by_turn),
                pl.BlockSpec((1, 1, 8, width), by_turn),
                pl.BlockSpec((1, 1, tokens, heads), lambda s, g, _: (s, g, 0, 0)),
            ],
        ),
        out_shape=[
            jax.ShapeDtypeStruct((groups, sessions, state, width), f32),
            jax.ShapeDtypeStruct((groups, sessions, 8, width), f32),
            jax.ShapeDtypeStruct((sessions, groups, tokens, heads), f32),
        ],
        compiler_params=pltpu.CompilerParams(vmem_limit_bytes=VMEM),
        cost_estimate=pl.CostEstimate(
            flops=2 * 10**9, bytes_accessed=8 * 2**20, transcendentals=2**18
        ),
        name="end_part",
    )(limits, x, b, raw, bias[:, :, None], rate[:, :, None])


def inside_part(limits, x, b, c, raw, bias, rate, skip):
    sessions, tokens, inner = x.shape
    groups = b.shape[1]
    flat, proj, per_token, per_head, per_channel = local_specs(x, b, raw)
    return pl.pallas_call(
        inside_kernel,
        grid_spec=pltpu.PrefetchScalarGridSpec(
            num_scalar_prefetch=1,
            grid=(sessions, groups),
            in_specs=[flat, proj, proj, per_token, per_head, per_head, per_channel],
            out_specs=flat,
        ),
        out_shape=jax.ShapeDtypeStruct((sessions, tokens, inner), jnp.float32),
        compiler_params=pltpu.CompilerParams(vmem_limit_bytes=VMEM),
        cost_estimate=pl.CostEstimate(
            flops=4 * 10**9, bytes_accessed=8 * 2**20, transcendentals=2**22
        ),
        name="inside_part",
    )(limits, x, b, c, raw, bias[:, :, None], rate[:, :, None], skip)


def leave_kernel(count, kind, *refs):
    at_ref, refs = refs[0], refs[1:]
    keep_ref, end_ref, state_ref, leaving_ref = refs[-4:]
    state = None
    if kind != "only":
        state = refs[0][0].astype(jnp.float32)
        refs = refs[1:]
    if count:
        first = jnp.concatenate([r[0, 0].astype(jnp.float32) for r in refs[:count]], axis=0)
        state = first if state is None else jnp.where(at_ref[1] == 0, first, state)
    state_ref[0] = state.astype(jnp.bfloat16)
    leaving_ref[0] = (keep_ref[0, 0, :1] * state + end_ref[0, 0]).astype(jnp.bfloat16)


def leave_part(at, coming, first, inside, keep, end):
    groups, sessions, state_size, width = end.shape
    by_turn = lambda s, at: (at[0], s, 0, 0)
    whole = pl.BlockSpec((1, state_size, width), lambda s, at: (s, 0, 0))
    operands, specs = [], []
    if coming is not None:
        operands.append(coming)
        specs.append(whole)
    if first is not None:
        operands += first
        specs += [
            pl.BlockSpec((1, 1, *f.shape[2:]), lambda s, at: (inside, s, 0, 0)) for f in first
        ]
    operands += [keep, end]
    specs += [
        pl.BlockSpec((1, 1, *keep.shape[2:]), by_turn),
        pl.BlockSpec((1, 1, state_size, width), by_turn),
    ]
    kind = None if first is None else ("only" if coming is None else "both")
    shape = jax.ShapeDtypeStruct((sessions, state_size, width), jnp.bfloat16)
    return pl.pallas_call(
        functools.partial(leave_kernel, 0 if first is None else len(first), kind),
        grid_spec=pltpu.PrefetchScalarGridSpec(
            num_scalar_prefetch=1, grid=(sessions,), in_specs=specs, out_specs=[whole, whole]
        ),
        out_shape=[shape, shape],
        compiler_params=pltpu.CompilerParams(vmem_limit_bytes=VMEM),
        cost_estimate=pl.CostEstimate(flops=10**6, bytes_accessed=3 * 2**20, transcendentals=0),
        name="leave_part",
    )(at, *operands)


def normed_kernel(at_ref, state_ref, c_ref, grow_ref, y_ref, gate_ref, gain_ref, _, out_ref):
    width = y_ref.shape[2]
    heads = grow_ref.shape[3]
    from_state = jnp.dot(c_ref[0, 0], state_ref[0], preferred_element_type=jnp.float32)
    ssd_out = y_ref[0] + from_state * spread(grow_ref[0, 0], width // heads)
    gate = gate_ref[0].astype(jnp.float32)
    gated = ssd_out * (gate / (1.0 + jnp.exp(-gate)))
    scale = lax.rsqrt(jnp.mean(gated * gated, axis=1, keepdims=True) + norm_eps)
    out_ref[0, 0] = (gated * scale * gain_ref[0]).astype(jnp.bfloat16)


def normed_part(index, at, state, c, grow, y, gate, gain, normed):
    sessions, tokens, inner = y.shape
    groups, state_size = c.shape[1], c.shape[3]
    width = inner // groups
    heads = grow.shape[3]
    by_both = lambda s, at: (s, at[0], 0, 0)
    flat = pl.BlockSpec((1, tokens, width), lambda s, at: (s, 0, at[0]))
    return pl.pallas_call(
        normed_kernel,
        grid_spec=pltpu.PrefetchScalarGridSpec(
            num_scalar_prefetch=1,
            grid=(sessions,),
            in_specs=[
                pl.BlockSpec((1, state_size, width), lambda s, at: (s, 0, 0)),
                pl.BlockSpec((1, 1, tokens, state_size), by_both),
                pl.BlockSpec((1, 1, tokens, heads), by_both),
                flat,
                flat,
                pl.BlockSpec((1, 1, width), lambda s, at: (at[0], 0, 0)),
                pl.BlockSpec(memory_space=pl.ANY),
            ],
            out_specs=pl.BlockSpec((1, 1, tokens, width), lambda s, at: (index, s, 0, 0)),
        ),
        out_shape=jax.ShapeDtypeStruct(normed.shape, normed.dtype),
        input_output_aliases={7: 0},
        compiler_params=pltpu.CompilerParams(vmem_limit_bytes=VMEM),
        cost_estimate=pl.CostEstimate(
            flops=10**8, bytes_accessed=4 * 2**20, transcendentals=2**19
        ),
        name="normed_part",
    )(at, state, c, grow, y, gate, gain, normed)


def pick_kernel(slot_ref, pool_ref, out_ref):
    heads, cols, head_dim = pool_ref.shape[1:]
    groups = out_ref.shape[0]
    per = heads // groups
    for g in range(groups):
        held = [pool_ref[0, g * per + h] for h in range(per)]
        out_ref[g, 0] = jnp.concatenate(held, axis=1).astype(jnp.bfloat16)


def pick_part(asked, pool, groups):
    _, heads, cols, head_dim = pool.shape
    count = asked.shape[0]
    width = heads // groups * head_dim
    return pl.pallas_call(
        pick_kernel,
        grid_spec=pltpu.PrefetchScalarGridSpec(
            num_scalar_prefetch=1,
            grid=(count,),
            in_specs=[pl.BlockSpec((1, heads, cols, head_dim), lambda i, slot: (slot[i], 0, 0, 0))],
            out_specs=pl.BlockSpec((groups, 1, cols, width), lambda i, slot: (0, i, 0, 0)),
        ),
        out_shape=jax.ShapeDtypeStruct((groups, count, cols, width), jnp.bfloat16),
        compiler_params=pltpu.CompilerParams(vmem_limit_bytes=VMEM),
        name="pick_part",
    )(asked, pool)


def final_kernel(value_ref, out_ref):
    heads, _, head_dim = out_ref.shape[1:]
    value = value_ref[0, 0].astype(jnp.float32)
    for h in range(heads):
        out_ref[0, h] = value[:, h * head_dim : (h + 1) * head_dim]


def final_part(value, heads, head_dim):
    groups, sessions, cols, width = value.shape
    per = heads // groups
    return pl.pallas_call(
        final_kernel,
        grid=(sessions, groups),
        in_specs=[pl.BlockSpec((1, 1, cols, width), lambda s, g: (g, s, 0, 0))],
        out_specs=pl.BlockSpec((1, per, cols, head_dim), lambda s, g: (s, g, 0, 0)),
        out_shape=jax.ShapeDtypeStruct((sessions, heads, cols, head_dim), jnp.float32),
        compiler_params=pltpu.CompilerParams(vmem_limit_bytes=VMEM),
        name="final_part",
    )(value)


def product_kernel(block_ref, left_ref, *refs):
    weights, out_ref = refs[:-1], refs[-1]
    total = jnp.zeros(out_ref.shape, jnp.float32)
    for k, weight in enumerate(weights):
        total += jnp.dot(left_ref[k], weight[...], preferred_element_type=jnp.float32)
    out_ref[...] = total.astype(out_ref.dtype)


def product(blocks, left, gathered, row_at, part=(0, 1)):
    parts, tokens, rows = left.shape
    count = blocks.shape[0]
    cols = gathered.shape[1] // part[1]
    tile = min(cols, TILE)
    tiles = cols // tile
    ahead = part[0] * tiles

    def weight_spec(k):
        return pl.BlockSpec((rows, tile), lambda i, j, blocks: (row_at(k, blocks[i]), ahead + j))

    return pl.pallas_call(
        product_kernel,
        grid_spec=pltpu.PrefetchScalarGridSpec(
            num_scalar_prefetch=1,
            grid=(count, tiles),
            in_specs=[pl.BlockSpec((parts, tokens, rows), lambda i, j, _: (0, 0, 0))]
            + [weight_spec(k) for k in range(parts)],
            out_specs=pl.BlockSpec((tokens, tile), lambda i, j, _: (0, i * tiles + j)),
        ),
        out_shape=jax.ShapeDtypeStruct((tokens, count * cols), jnp.bfloat16),
        compiler_params=pltpu.CompilerParams(vmem_limit_bytes=VMEM),
        cost_estimate=pl.CostEstimate(
            flops=2 * tokens * parts * rows * cols * count,
            bytes_accessed=2 * (tokens * parts * rows + parts * rows * cols * count),
            transcendentals=0,
        ),
        name="product",
    )(blocks.astype(jnp.int32), left, *[gathered] * parts)


def shards(
    head_input,
    gate_input,
    state_in_proj,
    state_out_proj,
    step_raw,
    head_step_bias,
    decay_log,
    skip_gain,
    norm_gain,
    out_weight,
    pool_states,
    slot_map,
    span_lengths,
):
    turns = lax.axis_size("ctx")
    turn = lax.axis_index("ctx")
    lanes = lax.axis_size("groups")
    lane = lax.axis_index("groups")
    cores = lax.axis_size("sess")
    core = lax.axis_index("sess")
    head_count = lax.axis_size("head")
    head_index = lax.axis_index("head")
    sessions, tokens, inner = head_input.shape
    heads = step_raw.shape[2]
    head_dim = inner // heads
    slots = pool_states.shape[0]
    state_cols = pool_states.shape[3]
    groups = heads // GROUP_HEADS
    width = inner // groups
    bf16 = jnp.bfloat16

    carriers = lanes * cores
    rows = inner // carriers
    mine = lax.dynamic_slice_in_dim(out_weight, (lane * cores + core) * rows, rows, 0)
    gathered = lax.all_gather(mine, ("groups", "ctx", "sess"), axis=0, tiled=True)

    def row_at(k, q):
        return (k // cores * turns + q) * cores + k % cores

    def slots_of(which):
        return lax.dynamic_slice_in_dim(slot_map, which * sessions, sessions)

    own_slots = slots_of(core)
    asked = jnp.concatenate([slots_of((core - by) % cores) for by in range(cores)])
    picked = pick_part(asked % slots, pool_states.transpose(0, 1, 3, 2), groups)
    start = picked[:, :sessions]
    for by in range(1, cores):
        found = picked[:, by * sessions : (by + 1) * sessions]
        found = lax.ppermute(found, "sess", [(i, (i - by) % cores) for i in range(cores)])
        here = (own_slots // slots == (core + by) % cores)[None, :, None, None]
        start = jnp.where(here, found, start)
    entering = []
    for g in range(groups):
        part = start[g : g + 1]
        if g:
            part, entering[-1] = lax.optimization_barrier((part, entering[-1]))
        entering.append([part] + [lax.ppermute(part, "ctx", [(k, 0)]) for k in range(1, turns)])

    first_session = core * sessions
    own_lengths = lax.dynamic_slice_in_dim(span_lengths, first_session, sessions)
    limits = jnp.clip(own_lengths * SPAN - turn * tokens, 0, tokens)
    first_group = head_index * groups

    def grouped(proj):
        return lax.dynamic_slice_in_dim(proj, first_group, groups, 2).swapaxes(1, 2)

    b = grouped(state_in_proj)
    c = grouped(state_out_proj)
    raw = step_raw.swapaxes(1, 2).reshape(sessions, groups, GROUP_HEADS, tokens)
    skip = jnp.repeat(skip_gain, head_dim).reshape(groups, 1, width)
    gain = norm_gain.reshape(groups, 1, width)
    bias = head_step_bias.reshape(groups, GROUP_HEADS)
    rate = decay_log.reshape(groups, GROUP_HEADS)
    end, keep, grow = end_part(limits, head_input, b, raw, bias, rate)

    waves = groups + turns - 2
    normed = jnp.zeros((waves + 1, sessions, tokens, width), bf16)
    leavings = []
    coming = None
    for index in range(waves + 1):
        at = jnp.stack([jnp.clip(index - turn, 0, groups - 1), turn]).astype(jnp.int32)
        given = entering[index] if index < groups else None
        state, leaving = leave_part(at, coming, given, 0, keep, end)
        leavings.append(leaving)
        if index < waves:
            pairs = [(i, i + 1) for i in range(turns - 1) if 0 <= index - i < groups]
            coming = lax.ppermute(leaving, "ctx", pairs)
        if index == 0:
            x, state = lax.optimization_barrier((head_input, state))
            y = inside_part(limits, x, b, c, raw, bias, rate, skip)
        normed = normed_part(index, at, state, c, grow, y, gate_input, gain, normed)
        if index < waves:
            coming, normed = lax.optimization_barrier((coming, normed))

    final = jnp.stack(leavings[turns - 1 :])

    def moved(final, step):
        by = turns // 2 ** (step + 1)
        half = final.shape[2] // 2
        pairs = [(z, z - by) for z in range(turns) if (turns - 1 - z) % (2 * by) == 0]
        return lax.ppermute(final[:, :, :half], "ctx", pairs)

    def placed(final, got, step):
        by = turns // 2 ** (step + 1)
        half = final.shape[2] // 2
        return jnp.where((turns - 1 - turn) % (2 * by) == by, got, final[:, :, half:])

    steps = (turns - 1).bit_length()

    left = lax.dynamic_slice_in_dim(normed, turn, groups, 0)
    left = left.reshape(groups, sessions * tokens, width)
    if groups != carriers:
        left = left.transpose(1, 0, 2).reshape(sessions * tokens, carriers, rows)
        left = left.transpose(1, 0, 2)
    left, gathered = lax.optimization_barrier((left, gathered))
    live = (jnp.arange(tokens, dtype=jnp.int32)[None, :] < limits[:, None]).astype(jnp.float32)
    if head_count == 2:
        share = turns // 2
        theirs = []
        got = moved(final, 0)
        block = jnp.int32(0)
        for m, part in [(0, (0, 2)), (0, (1, 2))] + [(m, (0, 1)) for m in range(1, share)]:
            which = ((1 - head_index) * share + m).reshape(1)
            which, block = lax.optimization_barrier((which, block))
            block = product(which, left, gathered, row_at, part)
            theirs.append(lax.ppermute(block, "head", [(0, 1), (1, 0)]))
            if part == (1, 2):
                got, block = lax.optimization_barrier((got, block))
                final = placed(final, got, 0)
        ours = product(head_index * share + jnp.arange(share), left, gathered, row_at)
        for step in range(1, steps):
            got = moved(final, step)
            got, ours = lax.optimization_barrier((got, ours))
            final = placed(final, got, step)
        final = final_part(final, heads, head_dim)
        theirs, ours, final = lax.optimization_barrier((theirs, ours, final))
        summed = ours.astype(jnp.float32) + jnp.concatenate(theirs, axis=1).astype(jnp.float32)
        mixed = (summed * live.reshape(-1, 1)).astype(bf16).reshape(sessions, tokens, -1)
    else:
        for step in range(steps):
            final = placed(final, moved(final, step), step)
        final = final_part(final, heads, head_dim)
        partial = product(jnp.arange(turns), left, gathered, row_at)
        partial = partial.reshape(sessions, tokens, -1)
        summed = lax.psum_scatter(partial, "head", scatter_dimension=2, tiled=True).astype(
            jnp.float32
        )
        mixed = (summed * live[:, :, None]).astype(bf16)
    return (mixed, final.transpose(0, 1, 3, 2))


def solution(mesh):
    placed = (
        P(("groups", "sess"), "ctx", "head"),
        P(("groups", "sess"), "ctx", "head"),
        P(("groups", "sess"), "ctx", None, None),
        P(("groups", "sess"), "ctx", None, None),
        P(("groups", "sess"), "ctx", "head"),
        P("head"),
        P("head"),
        P("head"),
        P("head"),
        P("head", "ctx"),
        P(("groups", "sess"), "head", None, "ctx"),
        P("groups"),
        P("groups"),
    )
    return jax.shard_map(
        shards,
        mesh=mesh,
        in_specs=placed,
        out_specs=(
            P(("groups", "sess"), "ctx", "head"),
            P(("groups", "sess"), "head", None, "ctx"),
        ),
        check_vma=False,
    )
```

```python
import functools

import jax
import jax.numpy as jnp
from jax import lax
from jax.experimental import pallas as pl
from jax.experimental.pallas import tpu as pltpu
from jax.sharding import PartitionSpec as P

HEADS = 128
GROUPS = 8
SPAN = 128
GROUP_HEADS = HEADS // GROUPS
TILE = 512
VMEM = 20 * 1024 * 1024

norm_eps = 1e-05
far = -1e30


def spread(values, head_dim):
    heads = values.shape[1]
    high = values.astype(jnp.bfloat16)
    low = (values - high.astype(jnp.float32)).astype(jnp.bfloat16)
    both = jnp.concatenate([high, low], axis=1)
    row = lax.broadcasted_iota(jnp.int32, (2 * heads, heads * head_dim), 0)
    col = lax.broadcasted_iota(jnp.int32, (2 * heads, heads * head_dim), 1)
    ones = (col // head_dim == row % heads).astype(jnp.bfloat16)
    return jnp.dot(both, ones, preferred_element_type=jnp.float32)


def decays(limit_ref, raw_ref, bias_ref, rate_ref):
    heads, tokens = raw_ref.shape[2:]
    f32 = jnp.float32
    token = lax.broadcasted_iota(jnp.int32, (heads, tokens), 1)
    size = jax.nn.softplus(raw_ref[0, 0] + bias_ref[0])
    size = size * (token < limit_ref[pl.program_id(0)]).astype(f32)
    log_keep = -jnp.exp(rate_ref[0]) * size
    row = lax.broadcasted_iota(jnp.int32, (tokens, tokens), 0)
    col = lax.broadcasted_iota(jnp.int32, (tokens, tokens), 1)
    cum = jnp.dot(log_keep, (row <= col).astype(f32), precision=lax.Precision.HIGHEST)
    return size, cum, row >= col


def end_kernel(
    limit_ref, x_ref, b_ref, raw_ref, bias_ref, rate_ref, end_ref, keep_ref, grow_ref
):
    tokens, width = x_ref.shape[1:]
    heads = raw_ref.shape[2]
    head_dim = width // heads
    f32 = jnp.float32
    size, cum, _ = decays(limit_ref, raw_ref, bias_ref, rate_ref)
    last = cum[:, tokens - 1 : tokens]
    tail = spread((jnp.exp(last - cum) * size).T, head_dim)
    weighted = (tail * x_ref[0].astype(f32)).astype(jnp.bfloat16)
    b_t = b_ref[0, 0].astype(f32).T.astype(jnp.bfloat16)
    end_ref[0, 0] = jnp.dot(b_t, weighted, preferred_element_type=f32).astype(jnp.bfloat16)
    grow = jnp.exp(cum.T)
    keep_ref[0, 0] = spread(jnp.broadcast_to(grow[tokens - 1 :], (8, heads)), head_dim)
    grow_ref[0, 0] = grow


def inside_kernel(
    limit_ref, x_ref, b_ref, c_ref, raw_ref, bias_ref, rate_ref, skip_ref, y_ref
):
    tokens, width = x_ref.shape[1:]
    heads = raw_ref.shape[2]
    head_dim = width // heads
    f32 = jnp.float32
    size, cum, causal = decays(limit_ref, raw_ref, bias_ref, rate_ref)
    cum_t = cum.T
    shifted = cum - jnp.where(size > 0, jnp.log(jnp.where(size > 0, size, 1.0)), far)
    scores = lax.dot_general(
        c_ref[0, 0], b_ref[0, 0], (((1,), (1,)), ((), ())), preferred_element_type=f32
    )
    lane = lax.broadcasted_iota(jnp.int32, (tokens, 2 * head_dim), 1)
    for pair in range(heads // 2):
        decayed = []
        for head in (2 * pair, 2 * pair + 1):
            gap = cum_t[:, head : head + 1] - shifted[head : head + 1, :]
            decayed.append((scores * jnp.exp(jnp.where(causal, gap, far))).astype(jnp.bfloat16))
        here = pl.ds(pair * 2 * head_dim, 2 * head_dim)
        x = x_ref[0, :, here]
        zero = jnp.zeros_like(x)
        apart = jnp.concatenate(
            [jnp.where(lane < head_dim, x, zero), jnp.where(lane >= head_dim, x, zero)], axis=0
        )
        y = jnp.dot(jnp.concatenate(decayed, axis=1), apart, preferred_element_type=f32)
        y_ref[0, :, here] = y + skip_ref[0, :, here] * x.astype(f32)


def local_specs(x, b, raw):
    tokens, width = x.shape[1], x.shape[2] // b.shape[1]
    state, heads = b.shape[3], raw.shape[2]

    def by_group(*block):
        return pl.BlockSpec((1, *block), lambda s, g, _: (g, 0, 0))

    def by_both(*block):
        return pl.BlockSpec((1, 1, *block), lambda s, g, _: (s, g, 0, 0))

    flat = pl.BlockSpec((1, tokens, width), lambda s, g, _: (s, 0, g))
    return (
        flat,
        by_both(tokens, state),
        by_both(heads, tokens),
        by_group(heads, 1),
        by_group(1, width),
    )


def end_part(limits, x, b, raw, bias, rate):
    sessions, tokens, inner = x.shape
    groups, state, heads = b.shape[1], b.shape[3], raw.shape[2]
    width = inner // groups
    flat, proj, per_token, per_head, _ = local_specs(x, b, raw)
    f32 = jnp.float32
    by_turn = lambda s, g, _: (g, s, 0, 0)
    return pl.pallas_call(
        end_kernel,
        grid_spec=pltpu.PrefetchScalarGridSpec(
            num_scalar_prefetch=1,
            grid=(sessions, groups),
            in_specs=[flat, proj, per_token, per_head, per_head],
            out_specs=[
                pl.BlockSpec((1, 1, state, width), by_turn),
                pl.BlockSpec((1, 1, 8, width), by_turn),
                pl.BlockSpec((1, 1, tokens, heads), lambda s, g, _: (s, g, 0, 0)),
            ],
        ),
        out_shape=[
            jax.ShapeDtypeStruct((groups, sessions, state, width), jnp.bfloat16),
            jax.ShapeDtypeStruct((groups, sessions, 8, width), f32),
            jax.ShapeDtypeStruct((sessions, groups, tokens, heads), f32),
        ],
        compiler_params=pltpu.CompilerParams(vmem_limit_bytes=VMEM),
        cost_estimate=pl.CostEstimate(
            flops=2 * 10**9, bytes_accessed=8 * 2**20, transcendentals=2**18
        ),
        name="end_part",
    )(limits, x, b, raw, bias[:, :, None], rate[:, :, None])


def inside_part(limits, x, b, c, raw, bias, rate, skip):
    sessions, tokens, inner = x.shape
    groups = b.shape[1]
    flat, proj, per_token, per_head, per_channel = local_specs(x, b, raw)
    return pl.pallas_call(
        inside_kernel,
        grid_spec=pltpu.PrefetchScalarGridSpec(
            num_scalar_prefetch=1,
            grid=(sessions, groups),
            in_specs=[flat, proj, proj, per_token, per_head, per_head, per_channel],
            out_specs=flat,
        ),
        out_shape=jax.ShapeDtypeStruct((sessions, tokens, inner), jnp.float32),
        compiler_params=pltpu.CompilerParams(vmem_limit_bytes=VMEM),
        cost_estimate=pl.CostEstimate(
            flops=4 * 10**9, bytes_accessed=8 * 2**20, transcendentals=2**22
        ),
        name="inside_part",
    )(limits, x, b, c, raw, bias[:, :, None], rate[:, :, None], skip)


def leave_kernel(count, kind, *refs):
    at_ref, refs = refs[0], refs[1:]
    keep_ref, end_ref, state_ref, leaving_ref = refs[-4:]
    state = None
    if kind != "only":
        state = refs[0][0].astype(jnp.float32)
        refs = refs[1:]
    if count:
        first = jnp.concatenate([r[0, 0].astype(jnp.float32) for r in refs[:count]], axis=0)
        state = first if state is None else jnp.where(at_ref[1] == 0, first, state)
    state_ref[0] = state.astype(jnp.bfloat16)
    leaving_ref[0] = (keep_ref[0, 0, :1] * state + end_ref[0, 0].astype(jnp.float32)).astype(jnp.bfloat16)


def leave_part(at, coming, first, inside, keep, end):
    groups, sessions, state_size, width = end.shape
    by_turn = lambda s, at: (at[0], s, 0, 0)
    whole = pl.BlockSpec((1, state_size, width), lambda s, at: (s, 0, 0))
    operands, specs = [], []
    if coming is not None:
        operands.append(coming)
        specs.append(whole)
    if first is not None:
        operands += first
        specs += [
            pl.BlockSpec((1, 1, *f.shape[2:]), lambda s, at: (inside, s, 0, 0)) for f in first
        ]
    operands += [keep, end]
    specs += [
        pl.BlockSpec((1, 1, *keep.shape[2:]), by_turn),
        pl.BlockSpec((1, 1, state_size, width), by_turn),
    ]
    kind = None if first is None else ("only" if coming is None else "both")
    shape = jax.ShapeDtypeStruct((sessions, state_size, width), jnp.bfloat16)
    return pl.pallas_call(
        functools.partial(leave_kernel, 0 if first is None else len(first), kind),
        grid_spec=pltpu.PrefetchScalarGridSpec(
            num_scalar_prefetch=1, grid=(sessions,), in_specs=specs, out_specs=[whole, whole]
        ),
        out_shape=[shape, shape],
        compiler_params=pltpu.CompilerParams(vmem_limit_bytes=VMEM),
        cost_estimate=pl.CostEstimate(flops=10**6, bytes_accessed=3 * 2**20, transcendentals=0),
        name="leave_part",
    )(at, *operands)


def normed_kernel(at_ref, state_ref, c_ref, grow_ref, y_ref, gate_ref, gain_ref, _, out_ref):
    width = y_ref.shape[2]
    heads = grow_ref.shape[3]
    from_state = jnp.dot(c_ref[0, 0], state_ref[0], preferred_element_type=jnp.float32)
    ssd_out = y_ref[0] + from_state * spread(grow_ref[0, 0], width // heads)
    gate = gate_ref[0].astype(jnp.float32)
    gated = ssd_out * (gate / (1.0 + jnp.exp(-gate)))
    scale = lax.rsqrt(jnp.mean(gated * gated, axis=1, keepdims=True) + norm_eps)
    out_ref[0, 0] = (gated * scale * gain_ref[0]).astype(jnp.bfloat16)


def normed_part(index, at, state, c, grow, y, gate, gain, normed):
    sessions, tokens, inner = y.shape
    groups, state_size = c.shape[1], c.shape[3]
    width = inner // groups
    heads = grow.shape[3]
    by_both = lambda s, at: (s, at[0], 0, 0)
    flat = pl.BlockSpec((1, tokens, width), lambda s, at: (s, 0, at[0]))
    return pl.pallas_call(
        normed_kernel,
        grid_spec=pltpu.PrefetchScalarGridSpec(
            num_scalar_prefetch=1,
            grid=(sessions,),
            in_specs=[
                pl.BlockSpec((1, state_size, width), lambda s, at: (s, 0, 0)),
                pl.BlockSpec((1, 1, tokens, state_size), by_both),
                pl.BlockSpec((1, 1, tokens, heads), by_both),
                flat,
                flat,
                pl.BlockSpec((1, 1, width), lambda s, at: (at[0], 0, 0)),
                pl.BlockSpec(memory_space=pl.ANY),
            ],
            out_specs=pl.BlockSpec((1, 1, tokens, width), lambda s, at: (index, s, 0, 0)),
        ),
        out_shape=jax.ShapeDtypeStruct(normed.shape, normed.dtype),
        input_output_aliases={7: 0},
        compiler_params=pltpu.CompilerParams(vmem_limit_bytes=VMEM),
        cost_estimate=pl.CostEstimate(
            flops=10**8, bytes_accessed=4 * 2**20, transcendentals=2**19
        ),
        name="normed_part",
    )(at, state, c, grow, y, gate, gain, normed)


def pick_kernel(slot_ref, pool_ref, out_ref):
    heads, cols, head_dim = pool_ref.shape[1:]
    groups = out_ref.shape[0]
    per = heads // groups
    for g in range(groups):
        held = [pool_ref[0, g * per + h] for h in range(per)]
        out_ref[g, 0] = jnp.concatenate(held, axis=1).astype(jnp.bfloat16)


def pick_part(asked, pool, groups):
    _, heads, cols, head_dim = pool.shape
    count = asked.shape[0]
    width = heads // groups * head_dim
    return pl.pallas_call(
        pick_kernel,
        grid_spec=pltpu.PrefetchScalarGridSpec(
            num_scalar_prefetch=1,
            grid=(count,),
            in_specs=[pl.BlockSpec((1, heads, cols, head_dim), lambda i, slot: (slot[i], 0, 0, 0))],
            out_specs=pl.BlockSpec((groups, 1, cols, width), lambda i, slot: (0, i, 0, 0)),
        ),
        out_shape=jax.ShapeDtypeStruct((groups, count, cols, width), jnp.bfloat16),
        compiler_params=pltpu.CompilerParams(vmem_limit_bytes=VMEM),
        name="pick_part",
    )(asked, pool)


def final_kernel(value_ref, out_ref):
    heads, _, head_dim = out_ref.shape[1:]
    value = value_ref[0, 0].astype(jnp.float32)
    for h in range(heads):
        out_ref[0, h] = value[:, h * head_dim : (h + 1) * head_dim]


def final_part(value, heads, head_dim):
    groups, sessions, cols, width = value.shape
    per = heads // groups
    return pl.pallas_call(
        final_kernel,
        grid=(sessions, groups),
        in_specs=[pl.BlockSpec((1, 1, cols, width), lambda s, g: (g, s, 0, 0))],
        out_specs=pl.BlockSpec((1, per, cols, head_dim), lambda s, g: (s, g, 0, 0)),
        out_shape=jax.ShapeDtypeStruct((sessions, heads, cols, head_dim), jnp.float32),
        compiler_params=pltpu.CompilerParams(vmem_limit_bytes=VMEM),
        name="final_part",
    )(value)


def product_kernel(block_ref, left_ref, *refs):
    weights, out_ref = refs[:-1], refs[-1]
    total = jnp.zeros(out_ref.shape, jnp.float32)
    for k, weight in enumerate(weights):
        total += jnp.dot(left_ref[k], weight[...], preferred_element_type=jnp.float32)
    out_ref[...] = total.astype(out_ref.dtype)


def product(blocks, left, gathered, row_at, part=(0, 1)):
    parts, tokens, rows = left.shape
    count = blocks.shape[0]
    cols = gathered.shape[1] // part[1]
    tile = min(cols, TILE)
    tiles = cols // tile
    ahead = part[0] * tiles

    def weight_spec(k):
        return pl.BlockSpec((rows, tile), lambda i, j, blocks: (row_at(k, blocks[i]), ahead + j))

    return pl.pallas_call(
        product_kernel,
        grid_spec=pltpu.PrefetchScalarGridSpec(
            num_scalar_prefetch=1,
            grid=(count, tiles),
            in_specs=[pl.BlockSpec((parts, tokens, rows), lambda i, j, _: (0, 0, 0))]
            + [weight_spec(k) for k in range(parts)],
            out_specs=pl.BlockSpec((tokens, tile), lambda i, j, _: (0, i * tiles + j)),
        ),
        out_shape=jax.ShapeDtypeStruct((tokens, count * cols), jnp.bfloat16),
        compiler_params=pltpu.CompilerParams(vmem_limit_bytes=VMEM),
        cost_estimate=pl.CostEstimate(
            flops=2 * tokens * parts * rows * cols * count,
            bytes_accessed=2 * (tokens * parts * rows + parts * rows * cols * count),
            transcendentals=0,
        ),
        name="product",
    )(blocks.astype(jnp.int32), left, *[gathered] * parts)


def shards(
    head_input,
    gate_input,
    state_in_proj,
    state_out_proj,
    step_raw,
    head_step_bias,
    decay_log,
    skip_gain,
    norm_gain,
    out_weight,
    pool_states,
    slot_map,
    span_lengths,
):
    turns = lax.axis_size("ctx")
    turn = lax.axis_index("ctx")
    lanes = lax.axis_size("groups")
    lane = lax.axis_index("groups")
    cores = lax.axis_size("sess")
    core = lax.axis_index("sess")
    head_count = lax.axis_size("head")
    head_index = lax.axis_index("head")
    sessions, tokens, inner = head_input.shape
    heads = step_raw.shape[2]
    head_dim = inner // heads
    slots = pool_states.shape[0]
    state_cols = pool_states.shape[3]
    groups = heads // GROUP_HEADS
    width = inner // groups
    bf16 = jnp.bfloat16

    carriers = lanes * cores
    rows = inner // carriers
    mine = lax.dynamic_slice_in_dim(out_weight, (lane * cores + core) * rows, rows, 0)
    gathered = lax.all_gather(mine, ("groups", "ctx", "sess"), axis=0, tiled=True)

    def row_at(k, q):
        return (k // cores * turns + q) * cores + k % cores

    def slots_of(which):
        return lax.dynamic_slice_in_dim(slot_map, which * sessions, sessions)

    own_slots = slots_of(core)
    asked = jnp.concatenate([slots_of((core - by) % cores) for by in range(cores)])
    picked = pick_part(asked % slots, pool_states.transpose(0, 1, 3, 2), groups)
    start = picked[:, :sessions]
    for by in range(1, cores):
        found = picked[:, by * sessions : (by + 1) * sessions]
        found = lax.ppermute(found, "sess", [(i, (i - by) % cores) for i in range(cores)])
        here = (own_slots // slots == (core + by) % cores)[None, :, None, None]
        start = jnp.where(here, found, start)
    entering = []
    for g in range(groups):
        part = start[g : g + 1]
        if g:
            part, entering[-1] = lax.optimization_barrier((part, entering[-1]))
        entering.append([part] + [lax.ppermute(part, "ctx", [(k, 0)]) for k in range(1, turns)])

    first_session = core * sessions
    own_lengths = lax.dynamic_slice_in_dim(span_lengths, first_session, sessions)
    limits = jnp.clip(own_lengths * SPAN - turn * tokens, 0, tokens)
    first_group = head_index * groups

    def grouped(proj):
        return lax.dynamic_slice_in_dim(proj, first_group, groups, 2).swapaxes(1, 2)

    b = grouped(state_in_proj)
    c = grouped(state_out_proj)
    raw = step_raw.swapaxes(1, 2).reshape(sessions, groups, GROUP_HEADS, tokens)
    skip = jnp.repeat(skip_gain, head_dim).reshape(groups, 1, width)
    gain = norm_gain.reshape(groups, 1, width)
    bias = head_step_bias.reshape(groups, GROUP_HEADS)
    rate = decay_log.reshape(groups, GROUP_HEADS)
    end, keep, grow = end_part(limits, head_input, b, raw, bias, rate)

    waves = groups + turns - 2
    normed = jnp.zeros((waves + 1, sessions, tokens, width), bf16)
    leavings = []
    coming = None
    for index in range(waves + 1):
        at = jnp.stack([jnp.clip(index - turn, 0, groups - 1), turn]).astype(jnp.int32)
        given = entering[index] if index < groups else None
        state, leaving = leave_part(at, coming, given, 0, keep, end)
        leavings.append(leaving)
        if index < waves:
            pairs = [(i, i + 1) for i in range(turns - 1) if 0 <= index - i < groups]
            coming = lax.ppermute(leaving, "ctx", pairs)
        if index == 0:
            x, state = lax.optimization_barrier((head_input, state))
            y = inside_part(limits, x, b, c, raw, bias, rate, skip)
        normed = normed_part(index, at, state, c, grow, y, gate_input, gain, normed)
        if index < waves:
            coming, normed = lax.optimization_barrier((coming, normed))

    final = jnp.stack(leavings[turns - 1 :])

    def moved(final, step):
        by = turns // 2 ** (step + 1)
        half = final.shape[2] // 2
        pairs = [(z, z - by) for z in range(turns) if (turns - 1 - z) % (2 * by) == 0]
        return lax.ppermute(final[:, :, :half], "ctx", pairs)

    def placed(final, got, step):
        by = turns // 2 ** (step + 1)
        half = final.shape[2] // 2
        return jnp.where((turns - 1 - turn) % (2 * by) == by, got, final[:, :, half:])

    steps = (turns - 1).bit_length()

    left = lax.dynamic_slice_in_dim(normed, turn, groups, 0)
    left = left.reshape(groups, sessions * tokens, width)
    if groups != carriers:
        left = left.transpose(1, 0, 2).reshape(sessions * tokens, carriers, rows)
        left = left.transpose(1, 0, 2)
    left, gathered = lax.optimization_barrier((left, gathered))
    live = (jnp.arange(tokens, dtype=jnp.int32)[None, :] < limits[:, None]).astype(jnp.float32)
    if head_count == 2:
        share = turns // 2
        theirs = []
        got = moved(final, 0)
        block = jnp.int32(0)
        for m, part in [(0, (0, 4)), (0, (1, 4)), (0, (1, 2))] + [(m, (0, 1)) for m in range(1, share)]:
            which = ((1 - head_index) * share + m).reshape(1)
            which, block = lax.optimization_barrier((which, block))
            block = product(which, left, gathered, row_at, part)
            theirs.append(lax.ppermute(block, "head", [(0, 1), (1, 0)]))
            if part == (1, 2):
                got, block = lax.optimization_barrier((got, block))
                final = placed(final, got, 0)
        ours = product(head_index * share + jnp.arange(share), left, gathered, row_at)
        for step in range(1, steps):
            got = moved(final, step)
            got, ours = lax.optimization_barrier((got, ours))
            final = placed(final, got, step)
        final = final_part(final, heads, head_dim)
        theirs, ours, final = lax.optimization_barrier((theirs, ours, final))
        summed = ours.astype(jnp.float32) + jnp.concatenate(theirs, axis=1).astype(jnp.float32)
        mixed = (summed * live.reshape(-1, 1)).astype(bf16).reshape(sessions, tokens, -1)
    else:
        for step in range(steps):
            final = placed(final, moved(final, step), step)
        final = final_part(final, heads, head_dim)
        partial = product(jnp.arange(turns), left, gathered, row_at)
        partial = partial.reshape(sessions, tokens, -1)
        summed = lax.psum_scatter(partial, "head", scatter_dimension=2, tiled=True).astype(
            jnp.float32
        )
        mixed = (summed * live[:, :, None]).astype(bf16)
    return (mixed, final.transpose(0, 1, 3, 2))


def solution(mesh):
    placed = (
        P(("groups", "sess"), "ctx", "head"),
        P(("groups", "sess"), "ctx", "head"),
        P(("groups", "sess"), "ctx", None, None),
        P(("groups", "sess"), "ctx", None, None),
        P(("groups", "sess"), "ctx", "head"),
        P("head"),
        P("head"),
        P("head"),
        P("head"),
        P("head", "ctx"),
        P(("groups", "sess"), "head", None, "ctx"),
        P("groups"),
        P("groups"),
    )
    return jax.shard_map(
        shards,
        mesh=mesh,
        in_specs=placed,
        out_specs=(
            P(("groups", "sess"), "ctx", "head"),
            P(("groups", "sess"), "head", None, "ctx"),
        ),
        check_vma=False,
    )
```

```python
import functools

import jax
import jax.numpy as jnp
from jax import lax
from jax.experimental import pallas as pl
from jax.experimental.pallas import tpu as pltpu
from jax.sharding import PartitionSpec as P

HEADS = 128
GROUPS = 8
SPAN = 128
GROUP_HEADS = HEADS // GROUPS
TILE = 512
VMEM = 20 * 1024 * 1024

norm_eps = 1e-05
far = -1e30


def spread(values, head_dim):
    heads = values.shape[1]
    high = values.astype(jnp.bfloat16)
    low = (values - high.astype(jnp.float32)).astype(jnp.bfloat16)
    both = jnp.concatenate([high, low], axis=1)
    row = lax.broadcasted_iota(jnp.int32, (2 * heads, heads * head_dim), 0)
    col = lax.broadcasted_iota(jnp.int32, (2 * heads, heads * head_dim), 1)
    ones = (col // head_dim == row % heads).astype(jnp.bfloat16)
    return jnp.dot(both, ones, preferred_element_type=jnp.float32)


def decays(limit_ref, raw_ref, bias_ref, rate_ref):
    heads, tokens = raw_ref.shape[2:]
    f32 = jnp.float32
    token = lax.broadcasted_iota(jnp.int32, (heads, tokens), 1)
    size = jax.nn.softplus(raw_ref[0, 0] + bias_ref[0])
    size = size * (token < limit_ref[pl.program_id(0)]).astype(f32)
    log_keep = -jnp.exp(rate_ref[0]) * size
    row = lax.broadcasted_iota(jnp.int32, (tokens, tokens), 0)
    col = lax.broadcasted_iota(jnp.int32, (tokens, tokens), 1)
    cum = jnp.dot(log_keep, (row <= col).astype(f32), precision=lax.Precision.HIGHEST)
    return size, cum, row >= col


def end_kernel(
    limit_ref, x_ref, b_ref, raw_ref, bias_ref, rate_ref, end_ref, keep_ref, grow_ref
):
    tokens, width = x_ref.shape[1:]
    heads = raw_ref.shape[2]
    head_dim = width // heads
    f32 = jnp.float32
    size, cum, _ = decays(limit_ref, raw_ref, bias_ref, rate_ref)
    last = cum[:, tokens - 1 : tokens]
    tail = spread((jnp.exp(last - cum) * size).T, head_dim)
    weighted = (tail * x_ref[0].astype(f32)).astype(jnp.bfloat16)
    b_t = b_ref[0, 0].astype(f32).T.astype(jnp.bfloat16)
    end_ref[0, 0] = jnp.dot(b_t, weighted, preferred_element_type=f32).astype(jnp.bfloat16)
    grow = jnp.exp(cum.T)
    keep_ref[0, 0] = spread(jnp.broadcast_to(grow[tokens - 1 :], (8, heads)), head_dim)
    grow_ref[0, 0] = grow


def inside_kernel(
    limit_ref, x_ref, b_ref, c_ref, raw_ref, bias_ref, rate_ref, skip_ref, y_ref
):
    tokens, width = x_ref.shape[1:]
    heads = raw_ref.shape[2]
    head_dim = width // heads
    f32 = jnp.float32
    size, cum, causal = decays(limit_ref, raw_ref, bias_ref, rate_ref)
    cum_t = cum.T
    shifted = cum - jnp.where(size > 0, jnp.log(jnp.where(size > 0, size, 1.0)), far)
    scores = lax.dot_general(
        c_ref[0, 0], b_ref[0, 0], (((1,), (1,)), ((), ())), preferred_element_type=f32
    )
    lane = lax.broadcasted_iota(jnp.int32, (tokens, 2 * head_dim), 1)
    for pair in range(heads // 2):
        decayed = []
        for head in (2 * pair, 2 * pair + 1):
            gap = cum_t[:, head : head + 1] - shifted[head : head + 1, :]
            decayed.append((scores * jnp.exp(jnp.where(causal, gap, far))).astype(jnp.bfloat16))
        here = pl.ds(pair * 2 * head_dim, 2 * head_dim)
        x = x_ref[0, :, here]
        zero = jnp.zeros_like(x)
        apart = jnp.concatenate(
            [jnp.where(lane < head_dim, x, zero), jnp.where(lane >= head_dim, x, zero)], axis=0
        )
        y = jnp.dot(jnp.concatenate(decayed, axis=1), apart, preferred_element_type=f32)
        y_ref[0, :, here] = y + skip_ref[0, :, here] * x.astype(f32)


def local_specs(x, b, raw):
    tokens, width = x.shape[1], x.shape[2] // b.shape[1]
    state, heads = b.shape[3], raw.shape[2]

    def by_group(*block):
        return pl.BlockSpec((1, *block), lambda s, g, _: (g, 0, 0))

    def by_both(*block):
        return pl.BlockSpec((1, 1, *block), lambda s, g, _: (s, g, 0, 0))

    flat = pl.BlockSpec((1, tokens, width), lambda s, g, _: (s, 0, g))
    return (
        flat,
        by_both(tokens, state),
        by_both(heads, tokens),
        by_group(heads, 1),
        by_group(1, width),
    )


def end_part(limits, x, b, raw, bias, rate):
    sessions, tokens, inner = x.shape
    groups, state, heads = b.shape[1], b.shape[3], raw.shape[2]
    width = inner // groups
    flat, proj, per_token, per_head, _ = local_specs(x, b, raw)
    f32 = jnp.float32
    by_turn = lambda s, g, _: (g, s, 0, 0)
    return pl.pallas_call(
        end_kernel,
        grid_spec=pltpu.PrefetchScalarGridSpec(
            num_scalar_prefetch=1,
            grid=(sessions, groups),
            in_specs=[flat, proj, per_token, per_head, per_head],
            out_specs=[
                pl.BlockSpec((1, 1, state, width), by_turn),
                pl.BlockSpec((1, 1, 8, width), by_turn),
                pl.BlockSpec((1, 1, tokens, heads), lambda s, g, _: (s, g, 0, 0)),
            ],
        ),
        out_shape=[
            jax.ShapeDtypeStruct((groups, sessions, state, width), jnp.bfloat16),
            jax.ShapeDtypeStruct((groups, sessions, 8, width), f32),
            jax.ShapeDtypeStruct((sessions, groups, tokens, heads), f32),
        ],
        compiler_params=pltpu.CompilerParams(vmem_limit_bytes=VMEM),
        cost_estimate=pl.CostEstimate(
            flops=2 * 10**9, bytes_accessed=8 * 2**20, transcendentals=2**18
        ),
        name="end_part",
    )(limits, x, b, raw, bias[:, :, None], rate[:, :, None])


def inside_part(limits, x, b, c, raw, bias, rate, skip):
    sessions, tokens, inner = x.shape
    groups = b.shape[1]
    flat, proj, per_token, per_head, per_channel = local_specs(x, b, raw)
    return pl.pallas_call(
        inside_kernel,
        grid_spec=pltpu.PrefetchScalarGridSpec(
            num_scalar_prefetch=1,
            grid=(sessions, groups),
            in_specs=[flat, proj, proj, per_token, per_head, per_head, per_channel],
            out_specs=flat,
        ),
        out_shape=jax.ShapeDtypeStruct((sessions, tokens, inner), jnp.float32),
        compiler_params=pltpu.CompilerParams(vmem_limit_bytes=VMEM),
        cost_estimate=pl.CostEstimate(
            flops=4 * 10**9, bytes_accessed=8 * 2**20, transcendentals=2**22
        ),
        name="inside_part",
    )(limits, x, b, c, raw, bias[:, :, None], rate[:, :, None], skip)


def leave_kernel(count, kind, *refs):
    at_ref, refs = refs[0], refs[1:]
    keep_ref, end_ref, state_ref, leaving_ref = refs[-4:]
    state = None
    if kind != "only":
        state = refs[0][0].astype(jnp.float32)
        refs = refs[1:]
    if count:
        first = jnp.concatenate([r[0, 0].astype(jnp.float32) for r in refs[:count]], axis=0)
        state = first if state is None else jnp.where(at_ref[1] == 0, first, state)
    state_ref[0] = state.astype(jnp.bfloat16)
    leaving_ref[0] = (keep_ref[0, 0, :1] * state + end_ref[0, 0].astype(jnp.float32)).astype(jnp.bfloat16)


def leave_part(at, coming, first, inside, keep, end):
    groups, sessions, state_size, width = end.shape
    by_turn = lambda s, at: (at[0], s, 0, 0)
    whole = pl.BlockSpec((1, state_size, width), lambda s, at: (s, 0, 0))
    operands, specs = [], []
    if coming is not None:
        operands.append(coming)
        specs.append(whole)
    if first is not None:
        operands += first
        specs += [
            pl.BlockSpec((1, 1, *f.shape[2:]), lambda s, at: (inside, s, 0, 0)) for f in first
        ]
    operands += [keep, end]
    specs += [
        pl.BlockSpec((1, 1, *keep.shape[2:]), by_turn),
        pl.BlockSpec((1, 1, state_size, width), by_turn),
    ]
    kind = None if first is None else ("only" if coming is None else "both")
    shape = jax.ShapeDtypeStruct((sessions, state_size, width), jnp.bfloat16)
    return pl.pallas_call(
        functools.partial(leave_kernel, 0 if first is None else len(first), kind),
        grid_spec=pltpu.PrefetchScalarGridSpec(
            num_scalar_prefetch=1, grid=(sessions,), in_specs=specs, out_specs=[whole, whole]
        ),
        out_shape=[shape, shape],
        compiler_params=pltpu.CompilerParams(vmem_limit_bytes=VMEM),
        cost_estimate=pl.CostEstimate(flops=10**6, bytes_accessed=3 * 2**20, transcendentals=0),
        name="leave_part",
    )(at, *operands)


def normed_kernel(at_ref, state_ref, c_ref, grow_ref, y_ref, gate_ref, gain_ref, _, out_ref):
    width = y_ref.shape[2]
    heads = grow_ref.shape[3]
    from_state = jnp.dot(c_ref[0, 0], state_ref[0], preferred_element_type=jnp.float32)
    ssd_out = y_ref[0] + from_state * spread(grow_ref[0, 0], width // heads)
    gate = gate_ref[0].astype(jnp.float32)
    gated = ssd_out * (gate / (1.0 + jnp.exp(-gate)))
    scale = lax.rsqrt(jnp.mean(gated * gated, axis=1, keepdims=True) + norm_eps)
    out_ref[0, 0] = (gated * scale * gain_ref[0]).astype(jnp.bfloat16)


def normed_part(index, at, state, c, grow, y, gate, gain, normed):
    sessions, tokens, inner = y.shape
    groups, state_size = c.shape[1], c.shape[3]
    width = inner // groups
    heads = grow.shape[3]
    by_both = lambda s, at: (s, at[0], 0, 0)
    flat = pl.BlockSpec((1, tokens, width), lambda s, at: (s, 0, at[0]))
    return pl.pallas_call(
        normed_kernel,
        grid_spec=pltpu.PrefetchScalarGridSpec(
            num_scalar_prefetch=1,
            grid=(sessions,),
            in_specs=[
                pl.BlockSpec((1, state_size, width), lambda s, at: (s, 0, 0)),
                pl.BlockSpec((1, 1, tokens, state_size), by_both),
                pl.BlockSpec((1, 1, tokens, heads), by_both),
                flat,
                flat,
                pl.BlockSpec((1, 1, width), lambda s, at: (at[0], 0, 0)),
                pl.BlockSpec(memory_space=pl.ANY),
            ],
            out_specs=pl.BlockSpec((1, 1, tokens, width), lambda s, at: (index, s, 0, 0)),
        ),
        out_shape=jax.ShapeDtypeStruct(normed.shape, normed.dtype),
        input_output_aliases={7: 0},
        compiler_params=pltpu.CompilerParams(vmem_limit_bytes=VMEM),
        cost_estimate=pl.CostEstimate(
            flops=10**8, bytes_accessed=4 * 2**20, transcendentals=2**19
        ),
        name="normed_part",
    )(at, state, c, grow, y, gate, gain, normed)


def pick_kernel(slot_ref, pool_ref, out_ref):
    heads, cols, head_dim = pool_ref.shape[1:]
    groups = out_ref.shape[0]
    per = heads // groups
    for g in range(groups):
        held = [pool_ref[0, g * per + h] for h in range(per)]
        out_ref[g, 0] = jnp.concatenate(held, axis=1).astype(jnp.bfloat16)


def pick_part(asked, pool, groups):
    _, heads, cols, head_dim = pool.shape
    count = asked.shape[0]
    width = heads // groups * head_dim
    return pl.pallas_call(
        pick_kernel,
        grid_spec=pltpu.PrefetchScalarGridSpec(
            num_scalar_prefetch=1,
            grid=(count,),
            in_specs=[pl.BlockSpec((1, heads, cols, head_dim), lambda i, slot: (slot[i], 0, 0, 0))],
            out_specs=pl.BlockSpec((groups, 1, cols, width), lambda i, slot: (0, i, 0, 0)),
        ),
        out_shape=jax.ShapeDtypeStruct((groups, count, cols, width), jnp.bfloat16),
        compiler_params=pltpu.CompilerParams(vmem_limit_bytes=VMEM),
        name="pick_part",
    )(asked, pool)


def final_kernel(value_ref, out_ref):
    heads, _, head_dim = out_ref.shape[1:]
    value = value_ref[0, 0].astype(jnp.float32)
    for h in range(heads):
        out_ref[0, h] = value[:, h * head_dim : (h + 1) * head_dim]


def final_part(value, heads, head_dim):
    groups, sessions, cols, width = value.shape
    per = heads // groups
    return pl.pallas_call(
        final_kernel,
        grid=(sessions, groups),
        in_specs=[pl.BlockSpec((1, 1, cols, width), lambda s, g: (g, s, 0, 0))],
        out_specs=pl.BlockSpec((1, per, cols, head_dim), lambda s, g: (s, g, 0, 0)),
        out_shape=jax.ShapeDtypeStruct((sessions, heads, cols, head_dim), jnp.float32),
        compiler_params=pltpu.CompilerParams(vmem_limit_bytes=VMEM),
        name="final_part",
    )(value)


def product_kernel(block_ref, left_ref, *refs):
    weights, out_ref = refs[:-1], refs[-1]
    total = jnp.zeros(out_ref.shape, jnp.float32)
    for k, weight in enumerate(weights):
        total += jnp.dot(left_ref[k], weight[...], preferred_element_type=jnp.float32)
    out_ref[...] = total.astype(out_ref.dtype)


def product(blocks, left, gathered, row_at, part=(0, 1)):
    parts, tokens, rows = left.shape
    count = blocks.shape[0]
    cols = gathered.shape[1] // part[1]
    tile = min(cols, TILE)
    tiles = cols // tile
    ahead = part[0] * tiles

    def weight_spec(k):
        return pl.BlockSpec((rows, tile), lambda i, j, blocks: (row_at(k, blocks[i]), ahead + j))

    return pl.pallas_call(
        product_kernel,
        grid_spec=pltpu.PrefetchScalarGridSpec(
            num_scalar_prefetch=1,
            grid=(count, tiles),
            in_specs=[pl.BlockSpec((parts, tokens, rows), lambda i, j, _: (0, 0, 0))]
            + [weight_spec(k) for k in range(parts)],
            out_specs=pl.BlockSpec((tokens, tile), lambda i, j, _: (0, i * tiles + j)),
        ),
        out_shape=jax.ShapeDtypeStruct((tokens, count * cols), jnp.bfloat16),
        compiler_params=pltpu.CompilerParams(vmem_limit_bytes=VMEM),
        cost_estimate=pl.CostEstimate(
            flops=2 * tokens * parts * rows * cols * count,
            bytes_accessed=2 * (tokens * parts * rows + parts * rows * cols * count),
            transcendentals=0,
        ),
        name="product",
    )(blocks.astype(jnp.int32), left, *[gathered] * parts)


def shards(
    head_input,
    gate_input,
    state_in_proj,
    state_out_proj,
    step_raw,
    head_step_bias,
    decay_log,
    skip_gain,
    norm_gain,
    out_weight,
    pool_states,
    slot_map,
    span_lengths,
):
    turns = lax.axis_size("ctx")
    turn = lax.axis_index("ctx")
    lanes = lax.axis_size("groups")
    lane = lax.axis_index("groups")
    cores = lax.axis_size("sess")
    core = lax.axis_index("sess")
    head_count = lax.axis_size("head")
    head_index = lax.axis_index("head")
    sessions, tokens, inner = head_input.shape
    heads = step_raw.shape[2]
    head_dim = inner // heads
    slots = pool_states.shape[0]
    state_cols = pool_states.shape[3]
    groups = heads // GROUP_HEADS
    width = inner // groups
    bf16 = jnp.bfloat16

    carriers = lanes * cores
    rows = inner // carriers
    mine = lax.dynamic_slice_in_dim(out_weight, (lane * cores + core) * rows, rows, 0)
    gathered = lax.all_gather(mine, ("groups", "ctx", "sess"), axis=0, tiled=True)

    def row_at(k, q):
        return (k // cores * turns + q) * cores + k % cores

    def slots_of(which):
        return lax.dynamic_slice_in_dim(slot_map, which * sessions, sessions)

    own_slots = slots_of(core)
    asked = jnp.concatenate([slots_of((core - by) % cores) for by in range(cores)])
    picked = pick_part(asked % slots, pool_states.transpose(0, 1, 3, 2), groups)
    start = picked[:, :sessions]
    for by in range(1, cores):
        found = picked[:, by * sessions : (by + 1) * sessions]
        found = lax.ppermute(found, "sess", [(i, (i - by) % cores) for i in range(cores)])
        here = (own_slots // slots == (core + by) % cores)[None, :, None, None]
        start = jnp.where(here, found, start)
    entering = []
    for g in range(groups):
        part = start[g : g + 1]
        if g:
            part, entering[-1] = lax.optimization_barrier((part, entering[-1]))
        entering.append([part] + [lax.ppermute(part, "ctx", [(k, 0)]) for k in range(1, turns)])

    first_session = core * sessions
    own_lengths = lax.dynamic_slice_in_dim(span_lengths, first_session, sessions)
    limits = jnp.clip(own_lengths * SPAN - turn * tokens, 0, tokens)
    first_group = head_index * groups

    def grouped(proj):
        return lax.dynamic_slice_in_dim(proj, first_group, groups, 2).swapaxes(1, 2)

    b = grouped(state_in_proj)
    c = grouped(state_out_proj)
    raw = step_raw.swapaxes(1, 2).reshape(sessions, groups, GROUP_HEADS, tokens)
    skip = jnp.repeat(skip_gain, head_dim).reshape(groups, 1, width)
    gain = norm_gain.reshape(groups, 1, width)
    bias = head_step_bias.reshape(groups, GROUP_HEADS)
    rate = decay_log.reshape(groups, GROUP_HEADS)
    end, keep, grow = end_part(limits, head_input, b, raw, bias, rate)

    waves = groups + turns - 2
    normed = jnp.zeros((waves + 1, sessions, tokens, width), bf16)
    leavings = []
    coming = None
    for index in range(waves + 1):
        at = jnp.stack([jnp.clip(index - turn, 0, groups - 1), turn]).astype(jnp.int32)
        given = entering[index] if index < groups else None
        state, leaving = leave_part(at, coming, given, 0, keep, end)
        leavings.append(leaving)
        if index < waves:
            pairs = [(i, i + 1) for i in range(turns - 1) if 0 <= index - i < groups]
            coming = lax.ppermute(leaving, "ctx", pairs)
        if index == 0:
            x, state = lax.optimization_barrier((head_input, state))
            y = inside_part(limits, x, b, c, raw, bias, rate, skip)
        normed = normed_part(index, at, state, c, grow, y, gate_input, gain, normed)
        if index < waves:
            coming, normed = lax.optimization_barrier((coming, normed))

    final = jnp.stack(leavings[turns - 1 :])

    def moved(final, step):
        by = turns // 2 ** (step + 1)
        half = final.shape[2] // 2
        pairs = [(z, z - by) for z in range(turns) if (turns - 1 - z) % (2 * by) == 0]
        return lax.ppermute(final[:, :, :half], "ctx", pairs)

    def placed(final, got, step):
        by = turns // 2 ** (step + 1)
        half = final.shape[2] // 2
        return jnp.where((turns - 1 - turn) % (2 * by) == by, got, final[:, :, half:])

    steps = (turns - 1).bit_length()

    left = lax.dynamic_slice_in_dim(normed, turn, groups, 0)
    left = left.reshape(groups, sessions * tokens, width)
    if groups != carriers:
        left = left.transpose(1, 0, 2).reshape(sessions * tokens, carriers, rows)
        left = left.transpose(1, 0, 2)
    left, gathered = lax.optimization_barrier((left, gathered))
    live = (jnp.arange(tokens, dtype=jnp.int32)[None, :] < limits[:, None]).astype(jnp.float32)
    if head_count == 2:
        share = turns // 2
        theirs = []
        got = moved(final, 0)
        block = jnp.int32(0)
        for m, part in [(0, (0, 2)), (0, (1, 2))] + [(m, (0, 1)) for m in range(1, share)]:
            which = ((1 - head_index) * share + m).reshape(1)
            which, block = lax.optimization_barrier((which, block))
            block = product(which, left, gathered, row_at, part)
            theirs.append(lax.ppermute(block, "head", [(0, 1), (1, 0)]))
            if part == (1, 2):
                got, block = lax.optimization_barrier((got, block))
                final = placed(final, got, 0)
        ours = product(head_index * share + jnp.arange(share), left, gathered, row_at)
        for step in range(1, steps):
            got = moved(final, step)
            got, ours = lax.optimization_barrier((got, ours))
            final = placed(final, got, step)
        final = final_part(final, heads, head_dim)
        theirs, ours, final = lax.optimization_barrier((theirs, ours, final))
        summed = ours.astype(jnp.float32) + jnp.concatenate(theirs, axis=1).astype(jnp.float32)
        mixed = (summed * live.reshape(-1, 1)).astype(bf16).reshape(sessions, tokens, -1)
    else:
        for step in range(steps):
            final = placed(final, moved(final, step), step)
        final = final_part(final, heads, head_dim)
        partial = product(jnp.arange(turns), left, gathered, row_at)
        partial = partial.reshape(sessions, tokens, -1)
        summed = lax.psum_scatter(partial, "head", scatter_dimension=2, tiled=True).astype(
            jnp.float32
        )
        mixed = (summed * live[:, :, None]).astype(bf16)
    return (mixed, final.transpose(0, 1, 3, 2))


def solution(mesh):
    placed = (
        P(("groups", "sess"), "ctx", "head"),
        P(("groups", "sess"), "ctx", "head"),
        P(("groups", "sess"), "ctx", None, None),
        P(("groups", "sess"), "ctx", None, None),
        P(("groups", "sess"), "ctx", "head"),
        P("head"),
        P("head"),
        P("head"),
        P("head"),
        P("head", "ctx"),
        P(("groups", "sess"), "head", None, "ctx"),
        P("groups"),
        P("groups"),
    )
    return jax.shard_map(
        shards,
        mesh=mesh,
        in_specs=placed,
        out_specs=(
            P(("groups", "sess"), "ctx", "head"),
            P(("groups", "sess"), "head", None, "ctx"),
        ),
        check_vma=False,
    )
```
